128 devices in a mesh: spec: 8 (over x_hi, y), neuron: 16 (over x_lo, z, core).
Axes of the slice: x: 4 (x_hi: 2, x_lo: 2; x = x_hi * 2 + x_lo), y: 4, z: 4, core: 2. Of those that a mesh axis runs over, the one named last changes fastest.
Arguments:
- panel: float32 [1536, 16384], P('spec', 'neuron'), may hold values from -6 to 6
- weight: float32 [16384, 16384], P('neuron', 'spec'), may hold values from -0.046875 to 0.046875
- layer_bias: float32 [16384], P('neuron'), may hold values from -0.06 to 0.06
- act_center: float32 [2, 16384], P(None, 'neuron'), may hold values from -6 to 6
- act_radius: float32 [2, 16384], P(None, 'neuron'), may hold values from 0.05 to 1
- alpha: float32 [2, 16384], P(None, 'neuron'), may hold values from 0 to 1
- in_center: float32 [2, 16384], P(None, 'spec'), may hold values from -0.12 to 0.12
- in_radius: float32 [2, 16384], P(None, 'spec'), may hold values from 1e-07 to 0.005
- bias_in: float32 [1536], replicated, may hold values from -6 to 6
- spec_neuron: int32 [2, 384], replicated, may hold values from 0 to 16383, as said below
- prior_lower: float32 [2, 16384], P(None, 'neuron'), may hold values from -7 to 0.5
- prior_upper: float32 [2, 16384], P(None, 'neuron'), may hold values from -0.5 to 7
Outputs:
- coef_next: float32 [1536, 16384], P('neuron', 'spec')
- lower_bound: float32 [1536], P('neuron')
- new_slope: float32 [2, 16384], P(None, 'neuron')
- new_shift: float32 [2, 16384], P(None, 'neuron')
The draws below stay inside these ranges and needn't reach their ends.
Inputs may be any that keep to these rules, and one draw needn't show every extreme that they name: `spec_neuron`: each sample's row names 384 different neurons.
All inputs are finite; a program needn't handle non-finite values.
Results may differ from the reference program's by a relative error of at most 0.0003.
Values sent between devices are 32-bit elements; how exact they have to be, the bound alone decides.
A program may use at most 128 MiB of HBM per device.

```python
import math
import jax
import jax.numpy as jnp
from jax import lax

WIDTH = 16384
SPECS = 384
ROWS = 1536


def draw_spec_neuron(key, part):
    key = jax.random.fold_in(key, 7)
    first = jax.random.permutation(jax.random.fold_in(key, 0), WIDTH)[:SPECS]
    second = jax.random.permutation(jax.random.fold_in(key, 1), WIDTH)[:SPECS]
    return jnp.stack([first, second]).astype(jnp.int32)


def level_of(own_key, extent, pieces, smallest, largest):
    def one(position, parts):
        draws = jax.random.uniform(jax.random.fold_in(jax.random.fold_in(own_key, 6), position), (parts,), jnp.float32, smallest / len(pieces), largest / len(pieces))
        return jnp.repeat(jnp.exp(draws), extent[position] // parts).reshape((-1,) + (1,) * (len(extent) - position - 1))

    gain = one(*pieces[0])
    for cut in pieces[1:]:
        gain = gain * one(*cut)
    return gain


def noise(own_key, dims, width, bound, cuts=(), kind=jnp.bfloat16):
    result = width * jax.random.normal(own_key, dims, jnp.float32)
    if cuts:
        result = result * level_of(own_key, dims, cuts, -0.22, 0.18)
    return jnp.clip(result, -bound, bound).astype(kind)


def setup_inputs(seed: int = 0) -> dict:
    streams_of = jax.random.split(jax.random.key(seed), 13)
    panel = noise(streams_of[0], (ROWS, WIDTH), 1.0, 6.0, ((0, 8), (1, 16)), jnp.float32)
    weight = noise(streams_of[1], (WIDTH, WIDTH), WIDTH ** -0.5, 0.046875, ((0, 16), (1, 8)), jnp.float32)
    layer_bias = noise(streams_of[2], (WIDTH,), 0.01, 0.06, ((0, 16),), jnp.float32)
    act_center = noise(streams_of[3], (2, WIDTH), 1.0, 6.0, ((1, 16),), jnp.float32)
    act_radius = jnp.clip(jnp.exp(math.log(1.0) - 2.9957323 * jax.random.uniform(streams_of[4], (2, WIDTH), jnp.float32) ** level_of(streams_of[4], (2, WIDTH), ((1, 16),), -0.2, 0.2)), 0.05, 1.0)
    alpha = jnp.clip(1.0 * jax.random.uniform(streams_of[5], (2, WIDTH), jnp.float32) ** level_of(streams_of[5], (2, WIDTH), ((1, 16),), -0.2, 0.2), 0.0, 1.0)
    in_center = noise(streams_of[6], (2, WIDTH), 0.02, 0.12, ((1, 8),), jnp.float32)
    in_radius = jnp.clip(jnp.exp(math.log(0.005) - 10.819778 * jax.random.uniform(streams_of[7], (2, WIDTH), jnp.float32) ** level_of(streams_of[7], (2, WIDTH), ((1, 8),), -0.2, 0.2)), 1.0000000116860974e-07, 0.005)
    bias_in = noise(streams_of[8], (ROWS,), 1.0, 6.0, (), jnp.float32)
    spec_neuron = draw_spec_neuron(jax.random.fold_in(streams_of[12], 71), 0)
    prior_lower = jnp.clip(-7.0 + 7.5 * jax.random.uniform(streams_of[10], (2, WIDTH), jnp.float32) ** level_of(streams_of[10], (2, WIDTH), ((1, 16),), -0.2, 0.2), -7.0, 0.5)
    prior_upper = jnp.clip(-0.5 + 7.5 * jax.random.uniform(streams_of[11], (2, WIDTH), jnp.float32) ** level_of(streams_of[11], (2, WIDTH), ((1, 16),), -0.2, 0.2), -0.5, 7.0)
    return dict(panel=panel, weight=weight, layer_bias=layer_bias, act_center=act_center, act_radius=act_radius, alpha=alpha, in_center=in_center, in_radius=in_radius, bias_in=bias_in, spec_neuron=spec_neuron, prior_lower=prior_lower, prior_upper=prior_upper)


def pick_rows(sample_table, row_sample):
    return jnp.where(row_sample[:, None] == 0, sample_table[0][None, :], sample_table[1][None, :])


def refresh_slope(new_low, new_high):
    rising = jax.nn.relu(new_high)
    falling = jax.nn.relu(-new_low)
    denom = rising + falling
    unstable = jnp.logical_and(new_low < 0.0, new_high > 0.0)
    safe = jnp.where(unstable, denom, 1.0)
    ratio = rising / safe
    slope = jnp.where(new_low >= 0.0, 1.0, jnp.where(new_high <= 0.0, 0.0, ratio))
    return slope, slope * falling


def reference(panel, weight, layer_bias, act_center, act_radius, alpha, in_center, in_radius, bias_in, spec_neuron, prior_lower, prior_upper):
    row_total = panel.shape[0]
    spec_count = spec_neuron.shape[1]
    row_sample = jnp.arange(row_total, dtype=jnp.int32) // (2 * spec_count)
    act_low = act_center - act_radius
    act_high = act_center + act_radius
    upper_part = jax.nn.relu(act_high)
    lower_part = jax.nn.relu(-act_low)
    up_slope = upper_part / (upper_part + lower_part)
    up_shift = up_slope * lower_part
    low_slope = jnp.where(act_low >= 0.0, 1.0, jnp.where(act_high <= 0.0, 0.0, alpha))
    relaxed = pick_rows(low_slope, row_sample) * jnp.maximum(panel, 0.0) + pick_rows(up_slope, row_sample) * jnp.minimum(panel, 0.0)
    shift_terms = jnp.dot(relaxed, layer_bias, precision=lax.Precision.HIGHEST, preferred_element_type=jnp.float32)
    shift_terms = shift_terms + jnp.sum(jnp.minimum(panel, 0.0) * pick_rows(up_shift, row_sample), axis=1)
    coef_next = jnp.dot(relaxed, weight, precision=lax.Precision.HIGHEST, preferred_element_type=jnp.float32)
    partial_sum = jnp.sum(coef_next * pick_rows(in_center, row_sample) - jnp.abs(coef_next) * pick_rows(in_radius, row_sample), axis=1)
    lower_bound = bias_in + shift_terms + partial_sum
    grouped = lower_bound.reshape(2, 2, spec_count)
    low_found = grouped[:, 0, :]
    high_found = -grouped[:, 1, :]
    sample_ids = jnp.arange(2, dtype=jnp.int32)[:, None]
    matched = jnp.zeros(prior_lower.shape, jnp.float32).at[sample_ids, spec_neuron].set(1.0)
    low_comp = jnp.zeros(prior_lower.shape, jnp.float32).at[sample_ids, spec_neuron].set(low_found)
    high_comp = jnp.zeros(prior_lower.shape, jnp.float32).at[sample_ids, spec_neuron].set(high_found)
    new_low = jnp.where(matched > 0, jnp.maximum(prior_lower, low_comp), prior_lower)
    new_high = jnp.where(matched > 0, jnp.minimum(prior_upper, high_comp), prior_upper)
    new_slope, new_shift = refresh_slope(new_low, new_high)
    return (coef_next, lower_bound, new_slope, new_shift)
```

```python
import functools

import jax
import jax.numpy as jnp
from jax import lax
from jax.experimental import pallas as pl
from jax.experimental.pallas import tpu as pltpu
from jax.sharding import PartitionSpec as P

MESH = pl.DeviceIdType.MESH
F32 = jnp.float32
BF16 = jnp.bfloat16
XH, Y, XL, Z = 2, 4, 2, 4
NSPEC, NNEUR = XH * Y, XL * Z * 2
LANES = 128

(S_XH, S_OWN_P, S_OWN_M, S_PAR_P, S_PAR_M, S_F0_P, S_F1_P, S_F0_M, S_F1_M,
 S_CORE, S_Z1_P, S_Z1_M, S_Z2_P, S_Z2_M, S_XL) = range(15)
NCOPY = 15

LOOK_XH = 4
LOOK_OWN = 3
LOOK_PAR = 2
TILE_N = 512
W_ROWS = 256


def fold_lanes(v):
    out = v[:, 0:LANES]
    for g in range(1, v.shape[1] // LANES):
        out = out + v[:, g * LANES:(g + 1) * LANES]
    return out


def rows_to_lanes(t):
    return lax.dot_general(
        jnp.ones((8, LANES), F32), t, (((1,), (1,)), ((), ())),
        precision=lax.Precision.HIGHEST, preferred_element_type=F32)


def kernel(panel, weight, lbias, ac, ar, al, ic, ir, bias, names, plow, phigh,
           coef, lbound, nslope, nshift,
           pan, wst, whi, wlo, g, asp, prod, cr, z1p, z1m, z2p, z2m, xb,
           ts, tb, shs, sb, ssum, pb, bb, onehot, touched,
           dsem, ssem, rsem, shs_s, shs_r, pb_s, pb_r, bb_s, bb_r):
    chunks = g.shape[0]
    kdim, ndim = whi.shape
    half = ndim // 2
    s = lax.axis_index("spec")
    n = lax.axis_index("neuron")
    xh, y = s // Y, s % Y
    xl, z, k = n // (2 * Z), (n // 2) % Z, n % 2
    yp, ym, y2 = (y + 1) % Y, (y + 3) % Y, (y + 2) % Y
    zp, zm, z2 = (z + 1) % Z, (z + 3) % Z, (z + 2) % Z

    dev_xh = ((1 - xh) * Y + y, n)
    dev_yp, dev_ym = (xh * Y + yp, n), (xh * Y + ym, n)
    dev_core = (s, xl * 2 * Z + z * 2 + (1 - k))
    dev_zp, dev_zm = (s, xl * 2 * Z + zp * 2 + k), (s, xl * 2 * Z + zm * 2 + k)
    dev_xl = (s, (1 - xl) * 2 * Z + z * 2 + k)

    load_panel = pltpu.make_async_copy(panel, pan, dsem.at[0])
    load_panel.start()
    pieces = kdim // W_ROWS
    w_loads = [
        pltpu.make_async_copy(weight.at[pl.ds(i * W_ROWS, W_ROWS)], wst.at[i], dsem.at[1 + i])
        for i in range(pieces)]
    for w_load in w_loads:
        w_load.start()

    barrier = pltpu.get_barrier_semaphore()
    for j in range(1, NSPEC):
        pl.semaphore_signal(barrier, inc=1, device_id=((s + j) % NSPEC, n), device_id_type=MESH)
    for j in range(1, NNEUR):
        pl.semaphore_signal(barrier, inc=1, device_id=(s, (n + j) % NNEUR), device_id_type=MESH)

    def pick(ref, i):
        return jnp.where(i == 0, ref[0:1, :], ref[1:2, :])

    center, radius = pick(ac, xh), pick(ar, xh)
    act_low, act_high = center - radius, center + radius
    upper, lower = jnp.maximum(act_high, 0.0), jnp.maximum(-act_low, 0.0)
    up_slope = upper / (upper + lower)
    up_shift = up_slope * lower
    low_slope = jnp.where(act_low >= 0.0, 1.0, jnp.where(act_high <= 0.0, 0.0, pick(al, xh)))
    lb = lbias[...]
    ts[...] = jnp.zeros_like(ts)
    tb[...] = jnp.zeros_like(tb)
    load_panel.wait()

    def relax(c, carry):
        for h in range(2):
            p = pan[h, pl.ds(pl.multiple_of(c * 8, 8), 8), :]
            neg = jnp.minimum(p, 0.0)
            rel = low_slope * jnp.maximum(p, 0.0) + up_slope * neg
            g[c, xh, y, h] = rel
            ts[h, pl.ds(pl.multiple_of(c * 8, 8), 8), :] = fold_lanes(rel * lb + neg * up_shift)
        return carry

    lax.fori_loop(0, chunks, relax, 0)
    pl.semaphore_wait(barrier, NSPEC + NNEUR - 2)

    def rc(src, dst, kind, c, dev):
        return pltpu.make_async_remote_copy(
            src_ref=src, dst_ref=dst, send_sem=ssem.at[c, kind], recv_sem=rsem.at[c, kind],
            device_id=dev, device_id_type=MESH)

    def block_copy(kind, c, bx, by, dev):
        return rc(g.at[c, bx, by], g.at[c, bx, by], kind, c, dev)

    def half_copy(kind, c, bx, by, h, dev):
        return rc(g.at[c, bx, by, h], g.at[c, bx, by, h], kind, c, dev)

    def xh_send(c): return block_copy(S_XH, c, xh, y, dev_xh)
    def xh_recv(c): return block_copy(S_XH, c, 1 - xh, y, dev_xh)

    def own_send(c):
        return [block_copy(S_OWN_P, c, xh, y, dev_yp), block_copy(S_OWN_M, c, xh, y, dev_ym)]

    def own_recv(c):
        return [block_copy(S_OWN_P, c, xh, ym, dev_yp), block_copy(S_OWN_M, c, xh, yp, dev_ym)]

    def par_send(c):
        return [block_copy(S_PAR_P, c, 1 - xh, y, dev_yp), block_copy(S_PAR_M, c, 1 - xh, y, dev_ym)]

    def par_recv(c):
        return [block_copy(S_PAR_P, c, 1 - xh, ym, dev_yp), block_copy(S_PAR_M, c, 1 - xh, yp, dev_ym)]

    def fwd_send(c):
        return [half_copy(S_F0_P, c, xh, ym, 0, dev_yp), half_copy(S_F0_M, c, xh, yp, 1, dev_ym),
                half_copy(S_F1_P, c, 1 - xh, ym, 0, dev_yp), half_copy(S_F1_M, c, 1 - xh, yp, 1, dev_ym)]

    def fwd_recv(c):
        return [half_copy(S_F0_P, c, xh, y2, 0, dev_yp), half_copy(S_F0_M, c, xh, y2, 1, dev_ym),
                half_copy(S_F1_P, c, 1 - xh, y2, 0, dev_yp), half_copy(S_F1_M, c, 1 - xh, y2, 1, dev_ym)]

    def core_copy(c):
        return rc(prod.at[c, :, :, 1 - k], cr.at[c], S_CORE, c, dev_core)

    def z1_copy(c):
        return [rc(prod.at[c, :, z2, k, :, pl.ds(0, half)], z1p.at[c], S_Z1_P, c, dev_zp),
                rc(prod.at[c, :, z2, k, :, pl.ds(half, half)], z1m.at[c], S_Z1_M, c, dev_zm)]

    def z2_copy(c):
        return [rc(prod.at[c, :, zp, k], z2p.at[c], S_Z2_P, c, dev_zp),
                rc(prod.at[c, :, zm, k], z2m.at[c], S_Z2_M, c, dev_zm)]

    def xl_copy(c):
        return rc(prod.at[c, 1 - xl, z, k], xb.at[c], S_XL, c, dev_xl)

    def start(copies):
        for copy in copies:
            copy.start()

    def wait_recv(copies):
        for copy in copies:
            copy.wait_recv()

    for c in range(min(LOOK_OWN, chunks)):
        xh_send(c).start()
        start(own_send(c))
    for c in range(LOOK_OWN, min(LOOK_XH, chunks)):
        xh_send(c).start()

    for h in range(2):
        shs[h] = rows_to_lanes(ts[h])

    def shs_copy(h):
        return pltpu.make_async_remote_copy(
            src_ref=shs.at[h], dst_ref=sb.at[n], send_sem=shs_s.at[h], recv_sem=shs_r.at[n],
            device_id=(s, 2 * s + h), device_id_type=MESH)

    for h in range(2):
        @pl.when(n != 2 * s + h)
        def _(h=h):
            shs_copy(h).start()

        @pl.when(n == 2 * s + h)
        def _(h=h):
            sb[n] = shs[h]

    def split_piece(i):
        def body(r, carry):
            w = wst[i, pl.ds(pl.multiple_of(r * 16, 16), 16), :]
            hi = w.astype(BF16)
            rows = pl.ds(pl.multiple_of(i * W_ROWS + r * 16, 16), 16)
            whi[rows, :] = hi
            wlo[rows, :] = (w - hi.astype(F32)).astype(BF16)
            return carry
        w_loads[i].wait()
        lax.fori_loop(0, W_ROWS // 16, body, 0)

    split_piece(0)
    for c in range(min(LOOK_PAR, chunks)):
        xh_recv(c).wait_recv()
        start(par_send(c))
        split_piece(1 + c)
    wait_recv(own_recv(0))
    wait_recv(par_recv(0))
    start(fwd_send(0))
    for i in range(1 + min(LOOK_PAR, chunks), pieces):
        split_piece(i)

    columns = (n * kdim).astype(F32)
    for b in range(2):
        found = jnp.zeros((8, kdim), F32)
        for q in range(4):
            row = jnp.broadcast_to(names[4 * b + q:4 * b + q + 1, :].astype(F32), (LANES, LANES))
            target = row.T - columns
            for t in range(kdim // LANES):
                ids = lax.broadcasted_iota(jnp.int32, (LANES, LANES), 1).astype(F32) + float(t * LANES)
                hit = jnp.where(target == ids, 1.0, 0.0)
                onehot[b, q * LANES:(q + 1) * LANES, t * LANES:(t + 1) * LANES] = hit.astype(BF16)
        total = jnp.zeros((8, kdim), F32)
        total = jnp.dot(jnp.ones((16, 4 * LANES), BF16), onehot[b], preferred_element_type=F32)
        touched[b:b + 1, :] = total[0:1, :]

    ssum[...] = jnp.zeros_like(ssum)

    @pl.when(n // 2 == s)
    def _():
        for j in range(1, NNEUR):
            other = (n + j) % NNEUR
            pltpu.make_async_remote_copy(
                src_ref=sb.at[other], dst_ref=sb.at[other], send_sem=shs_s.at[0],
                recv_sem=shs_r.at[other], device_id=(s, other), device_id_type=MESH).wait_recv()
        total = sb[0]
        for j in range(1, NNEUR):
            total = total + sb[j]
        ssum[...] = total

    in_center, in_radius = pick(ic, xl), pick(ir, xl)

    def multiply(c):
        a = g[c].reshape(16 * NSPEC, kdim)
        hi = a.astype(BF16)
        asp[0:16 * NSPEC, :] = hi
        asp[16 * NSPEC:, :] = (a - hi.astype(F32)).astype(BF16)

        def tile(j, carry):
            cols = pl.ds(pl.multiple_of(j * TILE_N, TILE_N), TILE_N)
            both = jnp.dot(asp[...], whi[:, cols], preferred_element_type=F32)
            rest = jnp.dot(asp[0:16 * NSPEC, :], wlo[:, cols], preferred_element_type=F32)
            res = both[0:16 * NSPEC] + both[16 * NSPEC:] + rest
            prod[c, :, :, :, :, cols] = res.reshape(XL, Z, 2, 8, TILE_N)
            return carry

        lax.fori_loop(0, ndim // TILE_N, tile, 0)

    def stage(cond, body):
        pl.when(cond)(body)

    def iteration(t, carry):
        @pl.when(t + LOOK_PAR < chunks)
        def _():
            c = t + LOOK_PAR
            xh_recv(c).wait_recv()
            start(par_send(c))

        @pl.when(t + LOOK_OWN < chunks)
        def _():
            start(own_send(t + LOOK_OWN))

        @pl.when(t + LOOK_XH < chunks)
        def _():
            xh_send(t + LOOK_XH).start()

        @pl.when(t + 1 < chunks)
        def _():
            wait_recv(own_recv(t + 1))
            wait_recv(par_recv(t + 1))
            start(fwd_send(t + 1))

        @pl.when(t < chunks)
        def _():
            wait_recv(fwd_recv(t))
            multiply(t)
            core_copy(t).start()

        @pl.when(jnp.logical_and(t >= 1, t - 1 < chunks))
        def _():
            c = t - 1
            wait_recv(z1_copy(c))
            for a in range(XL):
                prod[c, a, zp, k, :, 0:half] = (
                    prod[c, a, zp, k, :, 0:half] + cr[c, a, zp, :, 0:half] + z1p[c, a])
                prod[c, a, zp, k, :, half:] = prod[c, a, zp, k, :, half:] + cr[c, a, zp, :, half:]
                prod[c, a, zm, k, :, 0:half] = prod[c, a, zm, k, :, 0:half] + cr[c, a, zm, :, 0:half]
                prod[c, a, zm, k, :, half:] = (
                    prod[c, a, zm, k, :, half:] + cr[c, a, zm, :, half:] + z1m[c, a])
            start(z2_copy(c))

        @pl.when(jnp.logical_and(t >= 2, t - 2 < chunks))
        def _():
            c = t - 2
            wait_recv(z2_copy(c))
            for a in range(XL):
                prod[c, a, z, k] = prod[c, a, z, k] + cr[c, a, z] + z2p[c, a] + z2m[c, a]
            xl_copy(c).start()

        @pl.when(t >= 3)
        def _():
            c = t - 3
            xl_copy(c).wait_recv()
            v = prod[c, xl, z, k] + xb[c]
            rows = pl.ds(pl.multiple_of(c * 8, 8), 8)
            coef[rows, :] = v
            tb[rows, :] = fold_lanes(v * in_center - jnp.abs(v) * in_radius)

        @pl.when(t < chunks)
        def _():
            core_copy(t).wait_recv()
            for a in range(XL):
                prod[t, a, z2, k] = prod[t, a, z2, k] + cr[t, a, z2]
            start(z1_copy(t))

        return carry

    lax.fori_loop(0, chunks + 3, iteration, 0)

    pb[s] = rows_to_lanes(tb[...]) + ssum[...]

    def pb_copy(j, src):
        return pltpu.make_async_remote_copy(
            src_ref=pb.at[src], dst_ref=pb.at[src], send_sem=pb_s.at[j], recv_sem=pb_r.at[j],
            device_id=((s + j) % NSPEC, n), device_id_type=MESH)

    for j in range(1, NSPEC):
        pb_copy(j, s).start()
    for j in range(1, NSPEC):
        pb_copy(j, (s + NSPEC - j) % NSPEC).wait_recv()
    bound = pb[0]
    for j in range(1, NSPEC):
        bound = bound + pb[j]
    bound = bound + bias[pl.ds(n, 1), :]
    bb[n] = bound
    lbound[...] = bound[0:1, 0:lbound.shape[1]]

    def bb_copy(j, src):
        return pltpu.make_async_remote_copy(
            src_ref=bb.at[src], dst_ref=bb.at[src], send_sem=bb_s.at[j], recv_sem=bb_r.at[j],
            device_id=(s, (n + j) % NNEUR), device_id_type=MESH)

    for j in range(1, NNEUR):
        bb_copy(j, n).start()

    def drain(c, carry):
        xh_send(c).wait_send()
        core_copy(c).wait_send()
        xl_copy(c).wait_send()
        for copies in (own_send(c), par_send(c), fwd_send(c), z1_copy(c), z2_copy(c)):
            for copy in copies:
                copy.wait_send()
        return carry

    lax.fori_loop(0, chunks, drain, 0)
    for h in range(2):
        @pl.when(n != 2 * s + h)
        def _(h=h):
            shs_copy(h).wait_send()

    for j in range(1, NNEUR):
        bb_copy(j, (n + NNEUR - j) % NNEUR).wait_recv()

    row = lax.broadcasted_iota(jnp.int32, (8, 4 * LANES), 0)

    def parts(first):
        v = jnp.concatenate([bb[first + i] for i in range(4)], axis=1)
        p1 = v.astype(BF16).astype(F32)
        p2 = (v - p1).astype(BF16).astype(F32)
        p3 = v - p1 - p2
        return jnp.where(row == 0, p1, jnp.where(row == 1, p2, jnp.where(row == 2, p3, 0.0)))

    for b in range(2):
        lhs = jnp.concatenate([parts(8 * b), parts(8 * b + 4)], axis=0).astype(BF16)
        picked = jnp.dot(lhs, onehot[b], preferred_element_type=F32)
        low_found = jnp.sum(picked[0:8], axis=0, keepdims=True)
        high_found = -jnp.sum(picked[8:16], axis=0, keepdims=True)
        hit = touched[b:b + 1, :] > 0.0
        low0, high0 = plow[b:b + 1, :], phigh[b:b + 1, :]
        new_low = jnp.where(hit, jnp.maximum(low0, low_found), low0)
        new_high = jnp.where(hit, jnp.minimum(high0, high_found), high0)
        rising, falling = jnp.maximum(new_high, 0.0), jnp.maximum(-new_low, 0.0)
        unstable = jnp.logical_and(new_low < 0.0, new_high > 0.0)
        safe = jnp.where(unstable, rising + falling, 1.0)
        slope = jnp.where(new_low >= 0.0, 1.0, jnp.where(new_high <= 0.0, 0.0, rising / safe))
        nslope[b:b + 1, :] = slope
        nshift[b:b + 1, :] = slope * falling

    for j in range(1, NSPEC):
        pb_copy(j, s).wait_send()
    for j in range(1, NNEUR):
        bb_copy(j, n).wait_send()


def per_device(panel, weight, layer_bias, act_center, act_radius, alpha, in_center, in_radius,
               bias_in, spec_neuron, prior_lower, prior_upper):
    own_rows, kdim = panel.shape
    ndim = weight.shape[1]
    hrows = own_rows // 2
    chunks = hrows // 8
    spec_rows = bias_in.shape[0] // NNEUR
    names = jnp.pad(spec_neuron.reshape(8, -1), ((0, 0), (0, LANES - spec_rows)), constant_values=-1)
    bias = jnp.pad(bias_in.reshape(NNEUR, spec_rows), ((0, 0), (0, LANES - spec_rows)))
    vmem = pl.BlockSpec(memory_space=pltpu.VMEM)
    hbm = pl.BlockSpec(memory_space=pl.ANY)
    half = ndim // 2
    dma = pltpu.SemaphoreType.DMA
    coef, lbound, nslope, nshift = pl.pallas_call(
        kernel,
        out_shape=(
            jax.ShapeDtypeStruct((hrows, ndim), F32),
            jax.ShapeDtypeStruct((1, spec_rows), F32),
            jax.ShapeDtypeStruct((2, kdim), F32),
            jax.ShapeDtypeStruct((2, kdim), F32),
        ),
        in_specs=[hbm, hbm] + [vmem] * 10,
        out_specs=(vmem,) * 4,
        scratch_shapes=[
            pltpu.VMEM((2, hrows, kdim), F32),
            pltpu.VMEM((kdim // W_ROWS, W_ROWS, ndim), F32),
            pltpu.VMEM((kdim, ndim), BF16),
            pltpu.VMEM((kdim, ndim), BF16),
            pltpu.VMEM((chunks, XH, Y, 2, 8, kdim), F32),
            pltpu.VMEM((2 * 16 * NSPEC, kdim), BF16),
            pltpu.VMEM((chunks, XL, Z, 2, 8, ndim), F32),
            pltpu.VMEM((chunks, XL, Z, 8, ndim), F32),
            pltpu.VMEM((chunks, XL, 8, half), F32),
            pltpu.VMEM((chunks, XL, 8, half), F32),
            pltpu.VMEM((chunks, XL, 8, ndim), F32),
            pltpu.VMEM((chunks, XL, 8, ndim), F32),
            pltpu.VMEM((chunks, 8, ndim), F32),
            pltpu.VMEM((2, LANES, LANES), F32),
            pltpu.VMEM((LANES, LANES), F32),
            pltpu.VMEM((2, 8, LANES), F32),
            pltpu.VMEM((NNEUR, 8, LANES), F32),
            pltpu.VMEM((8, LANES), F32),
            pltpu.VMEM((NSPEC, 8, LANES), F32),
            pltpu.VMEM((NNEUR, 8, LANES), F32),
            pltpu.VMEM((2, 4 * LANES, kdim), BF16),
            pltpu.VMEM((2, kdim), F32),
            dma((1 + kdim // W_ROWS,)),
            dma((chunks, NCOPY)), dma((chunks, NCOPY)),
            dma((2,)), dma((NNEUR,)),
            dma((NSPEC,)), dma((NSPEC,)),
            dma((NNEUR,)), dma((NNEUR,)),
        ],
        compiler_params=pltpu.CompilerParams(
            collective_id=0, has_side_effects=True, vmem_limit_bytes=60 * 1024 * 1024),
        cost_estimate=pl.CostEstimate(
            flops=6 * 8 * own_rows * kdim * ndim, bytes_accessed=4 * kdim * ndim, transcendentals=0),
    )(panel.reshape(2, hrows, kdim), weight, layer_bias.reshape(1, kdim), act_center, act_radius,
      alpha, in_center, in_radius, bias, names, prior_lower, prior_upper)
    return coef, lbound.reshape(spec_rows), nslope, nshift


def solution(mesh):
    in_specs = (
        P("spec", "neuron"),
        P("neuron", "spec"),
        P("neuron"),
        P(None, "neuron"),
        P(None, "neuron"),
        P(None, "neuron"),
        P(None, "spec"),
        P(None, "spec"),
        P(),
        P(),
        P(None, "neuron"),
        P(None, "neuron"),
    )
    out_specs = (P("neuron", "spec"), P("neuron"), P(None, "neuron"), P(None, "neuron"))
    return jax.shard_map(
        per_device, mesh=mesh, in_specs=in_specs, out_specs=out_specs, check_vma=False
    )
```

```python
import functools

import jax
import jax.numpy as jnp
from jax import lax
from jax.experimental import pallas as pl
from jax.experimental.pallas import tpu as pltpu
from jax.sharding import PartitionSpec as P

MESH = pl.DeviceIdType.MESH
F32 = jnp.float32
BF16 = jnp.bfloat16
XH, Y, XL, Z = 2, 4, 2, 4
NSPEC, NNEUR = XH * Y, XL * Z * 2
LANES = 128

(S_XH, S_OWN_P, S_OWN_M, S_PAR_P, S_PAR_M, S_FWD_P, S_FWD_M,
 S_CORE, S_Z1_P, S_Z1_M, S_Z2_P, S_Z2_M, S_XL) = range(13)
NCOPY = 13

LAG_Z2 = 2
LAG_FIN = 4
LAG_OUT = 5
LOOK_XH = 4
LOOK_PAR = 2
TILE_N = 512
W_ROWS = 256


def fold_lanes(v):
    out = v[:, 0:LANES]
    for g in range(1, v.shape[1] // LANES):
        out = out + v[:, g * LANES:(g + 1) * LANES]
    return out


def rows_to_lanes(t):
    return lax.dot_general(
        jnp.ones((8, LANES), F32), t, (((1,), (1,)), ((), ())),
        precision=lax.Precision.HIGHEST, preferred_element_type=F32)


def kernel(panel, weight, *rest):
    small_in = rest[:10]
    coef = rest[10]
    lbound, nslope, nshift = rest[11:14]
    small = rest[14:24]
    body(panel, weight, small_in, small, coef, lbound, nslope, nshift, *rest[24:])


def body(panel, weight, small_in, small, coef, lbound, nslope, nshift,
           pan, wst, whi, wlo, g, asp, prod, cr, z1p, z1m, z2p, z2m, xb,
           ts, tb, shs, sb, pb, bb, onehot, touched, bias16, out,
           dsem, osem, ssem, rsem, shs_s, shs_r, pb_s, pb_r, bb_s, bb_r):
    chunks = g.shape[0]
    kdim, ndim = whi.shape
    half = ndim // 2
    s = lax.axis_index("spec")
    n = lax.axis_index("neuron")
    xh, y = s // Y, s % Y
    xl, z, k = n // (2 * Z), (n // 2) % Z, n % 2
    yp, ym, y2 = (y + 1) % Y, (y + 3) % Y, (y + 2) % Y
    zp, zm, z2 = (z + 1) % Z, (z + 3) % Z, (z + 2) % Z

    dev_xh = ((1 - xh) * Y + y, n)
    dev_yp, dev_ym = (xh * Y + yp, n), (xh * Y + ym, n)
    dev_core = (s, xl * 2 * Z + z * 2 + (1 - k))
    dev_zp, dev_zm = (s, xl * 2 * Z + zp * 2 + k), (s, xl * 2 * Z + zm * 2 + k)
    dev_xl = (s, (1 - xl) * 2 * Z + z * 2 + k)

    barrier = pltpu.get_barrier_semaphore()
    for j in range(1, NSPEC):
        pl.semaphore_signal(barrier, inc=1, device_id=((s + j) % NSPEC, n), device_id_type=MESH)
    for j in range(1, NNEUR):
        pl.semaphore_signal(barrier, inc=1, device_id=(s, (n + j) % NNEUR), device_id_type=MESH)

    loads = [pltpu.make_async_copy(a, b, dsem.at[i]) for i, (a, b) in enumerate(zip(small_in, small))]
    load_panel = pltpu.make_async_copy(panel, pan, dsem.at[10])
    for load in loads[:4]:
        load.start()
    load_panel.start()
    for load in loads[4:]:
        load.start()
    pieces = kdim // W_ROWS
    w_loads = [
        pltpu.make_async_copy(weight.at[pl.ds(i * W_ROWS, W_ROWS)], wst.at[i], dsem.at[11 + i])
        for i in range(pieces)]
    for w_load in w_loads:
        w_load.start()
    lbias, ac, ar, al, ic, ir, bias, names, plow, phigh = small

    for load in loads[:4]:
        load.wait()

    def pick(ref, i):
        return jnp.where(i == 0, ref[0:1, :], ref[1:2, :])

    center, radius = pick(ac, xh), pick(ar, xh)
    act_low, act_high = center - radius, center + radius
    upper, lower = jnp.maximum(act_high, 0.0), jnp.maximum(-act_low, 0.0)
    up_slope = upper / (upper + lower)
    up_shift = up_slope * lower
    low_slope = jnp.where(act_low >= 0.0, 1.0, jnp.where(act_high <= 0.0, 0.0, pick(al, xh)))
    lb = lbias[...]
    ts[...] = jnp.zeros_like(ts)
    tb[...] = jnp.zeros_like(tb)
    load_panel.wait()

    def relax(c, carry):
        for h in range(2):
            p = pan[h, pl.ds(pl.multiple_of(c * 8, 8), 8), :]
            neg = jnp.minimum(p, 0.0)
            rel = low_slope * jnp.maximum(p, 0.0) + up_slope * neg
            g[c, xh, y, h] = rel
            ts[h, pl.ds(pl.multiple_of(c * 8, 8), 8), :] = fold_lanes(rel * lb + neg * up_shift)
        return carry

    first = min(LOOK_PAR, chunks)
    lax.fori_loop(0, first, relax, 0)
    pl.semaphore_wait(barrier, NSPEC + NNEUR - 2)

    def rc(src, dst, kind, c, dev):
        return pltpu.make_async_remote_copy(
            src_ref=src, dst_ref=dst, send_sem=ssem.at[c, kind], recv_sem=rsem.at[c, kind],
            device_id=dev, device_id_type=MESH)

    def block_copy(kind, c, bx, by, dev):
        return rc(g.at[c, bx, by], g.at[c, bx, by], kind, c, dev)

    def pair_copy(kind, c, by, dev):
        return rc(g.at[c, :, by], g.at[c, :, by], kind, c, dev)

    def half_copy(kind, c, by, h, dev):
        return rc(g.at[c, :, by, h], g.at[c, :, by, h], kind, c, dev)

    def xh_send(c): return block_copy(S_XH, c, xh, y, dev_xh)
    def xh_recv(c): return block_copy(S_XH, c, 1 - xh, y, dev_xh)

    def own_send(c):
        return [block_copy(S_OWN_P, c, xh, y, dev_yp), block_copy(S_OWN_M, c, xh, y, dev_ym)]

    def own_recv(c):
        return [block_copy(S_OWN_P, c, xh, ym, dev_yp), block_copy(S_OWN_M, c, xh, yp, dev_ym)]

    def par_send(c):
        return [block_copy(S_PAR_P, c, 1 - xh, y, dev_yp), block_copy(S_PAR_M, c, 1 - xh, y, dev_ym)]

    def par_recv(c):
        return [block_copy(S_PAR_P, c, 1 - xh, ym, dev_yp), block_copy(S_PAR_M, c, 1 - xh, yp, dev_ym)]

    def pair_send(c):
        return [pair_copy(S_OWN_P, c, y, dev_yp), pair_copy(S_OWN_M, c, y, dev_ym)]

    def pair_recv(c):
        return [pair_copy(S_OWN_P, c, ym, dev_yp), pair_copy(S_OWN_M, c, yp, dev_ym)]

    def fwd_send(c):
        return [half_copy(S_FWD_P, c, ym, 0, dev_yp), half_copy(S_FWD_M, c, yp, 1, dev_ym)]

    def fwd_recv(c):
        return [half_copy(S_FWD_P, c, y2, 0, dev_yp), half_copy(S_FWD_M, c, y2, 1, dev_ym)]

    def core_copy(c):
        return rc(prod.at[c, :, :, 1 - k], cr.at[c], S_CORE, c, dev_core)

    def z1_copy(c):
        return [rc(prod.at[c, :, z2, k, :, pl.ds(0, half)], z1p.at[c], S_Z1_P, c, dev_zp),
                rc(prod.at[c, :, z2, k, :, pl.ds(half, half)], z1m.at[c], S_Z1_M, c, dev_zm)]

    def z2_copy(c):
        return [rc(prod.at[c, :, zp, k], z2p.at[c], S_Z2_P, c, dev_zp),
                rc(prod.at[c, :, zm, k], z2m.at[c], S_Z2_M, c, dev_zm)]

    def xl_copy(c):
        return rc(prod.at[c, 1 - xl, z, k], xb.at[c], S_XL, c, dev_xl)

    def out_copy(c):
        return pltpu.make_async_copy(
            out.at[c], coef.at[pl.ds(pl.multiple_of(c * 8, 8), 8)], osem.at[c])

    def start(copies):
        for copy in copies:
            copy.start()

    def wait_recv(copies):
        for copy in copies:
            copy.wait_recv()

    for c in range(first):
        xh_send(c).start()
        start(own_send(c))
    lax.fori_loop(first, chunks, relax, 0)
    for c in range(LOOK_PAR, min(LOOK_XH, chunks)):
        xh_send(c).start()

    for h in range(2):
        shs[h] = rows_to_lanes(ts[h])

    def shs_copy(h):
        return pltpu.make_async_remote_copy(
            src_ref=shs.at[h], dst_ref=sb.at[n], send_sem=shs_s.at[h], recv_sem=shs_r.at[n],
            device_id=(s, 2 * s + h), device_id_type=MESH)

    for h in range(2):
        @pl.when(n != 2 * s + h)
        def _(h=h):
            shs_copy(h).start()

        @pl.when(n == 2 * s + h)
        def _(h=h):
            sb[n] = shs[h]

    def split_piece(i):
        def body(r, carry):
            w = wst[i, pl.ds(pl.multiple_of(r * 16, 16), 16), :]
            hi = w.astype(BF16)
            rows = pl.ds(pl.multiple_of(i * W_ROWS + r * 16, 16), 16)
            whi[rows, :] = hi
            wlo[rows, :] = (w - hi.astype(F32)).astype(BF16)
            return carry
        w_loads[i].wait()
        lax.fori_loop(0, W_ROWS // 16, body, 0)

    split_piece(0)
    for c in range(min(LOOK_PAR, chunks)):
        xh_recv(c).wait_recv()
        start(par_send(c))
        split_piece(1 + c)
    wait_recv(own_recv(0))
    wait_recv(par_recv(0))
    start(fwd_send(0))
    for i in range(1 + min(LOOK_PAR, chunks), pieces):
        split_piece(i)

    for load in loads[4:]:
        load.wait()

    def row_piece(v, first, count):
        at = first // LANES * LANES
        if first % LANES == 0:
            return v[:, at:at + LANES]
        width = min(2 * LANES, v.shape[1] - at)
        return pltpu.roll(v[:, at:at + width], width - first % LANES, 1)[:, 0:LANES]

    spec_rows = lbound.shape[1]
    lane = lax.broadcasted_iota(jnp.int32, (1, LANES), 1)
    bias_row = jnp.concatenate([bias[i:i + 1, :] for i in range(bias.shape[0])], axis=1)
    for j in range(NNEUR):
        piece = row_piece(bias_row, j * spec_rows, spec_rows)
        bias16[j:j + 1, :] = jnp.where(lane < spec_rows, piece, 0.0)
    columns = (n * kdim).astype(F32)
    for b in range(2):
        for q in range(4):
            row = row_piece(names[b:b + 1, :].astype(F32), q * spec_rows, spec_rows)
            row = jnp.broadcast_to(jnp.where(lane < spec_rows, row, -1.0), (LANES, LANES))
            target = row.T - columns
            for t in range(kdim // LANES):
                ids = lax.broadcasted_iota(jnp.int32, (LANES, LANES), 1).astype(F32) + float(t * LANES)
                hit = jnp.where(target == ids, 1.0, 0.0)
                onehot[b, q * LANES:(q + 1) * LANES, t * LANES:(t + 1) * LANES] = hit.astype(BF16)
        total = jnp.dot(jnp.ones((16, 4 * LANES), BF16), onehot[b], preferred_element_type=F32)
        touched[b:b + 1, :] = total[0:1, :]

    def shift_recv():
        for j in range(1, NNEUR):
            other = (n + j) % NNEUR
            pltpu.make_async_remote_copy(
                src_ref=sb.at[other], dst_ref=sb.at[other], send_sem=shs_s.at[0],
                recv_sem=shs_r.at[other], device_id=(s, other), device_id_type=MESH).wait_recv()

    in_center, in_radius = pick(ic, xl), pick(ir, xl)
    row8 = lax.broadcasted_iota(jnp.int32, (8, LANES), 0)
    lane8 = lax.broadcasted_iota(jnp.int32, (8, LANES), 1)

    def multiply(c):
        a = g[c].reshape(16 * NSPEC, kdim)
        hi = a.astype(BF16)
        asp[0:16 * NSPEC, :] = hi
        asp[16 * NSPEC:, :] = (a - hi.astype(F32)).astype(BF16)

        def tile(j, carry):
            cols = pl.ds(pl.multiple_of(j * TILE_N, TILE_N), TILE_N)
            both = jnp.dot(asp[...], whi[:, cols], preferred_element_type=F32)
            rest = jnp.dot(asp[0:16 * NSPEC, :], wlo[:, cols], preferred_element_type=F32)
            res = both[0:16 * NSPEC] + both[16 * NSPEC:] + rest
            prod[c, :, :, :, :, cols] = res.reshape(XL, Z, 2, 8, TILE_N)
            return carry

        lax.fori_loop(0, ndim // TILE_N, tile, 0)

    def stage(cond, body):
        pl.when(cond)(body)

    def drain(c):
        xh_send(c).wait_send()
        core_copy(c).wait_send()
        xl_copy(c).wait_send()
        out_copy(c).wait()
        for copies in (fwd_send(c), z1_copy(c), z2_copy(c)):
            for copy in copies:
                copy.wait_send()

        @pl.when(c < LOOK_PAR)
        def _():
            for copy in own_send(c) + par_send(c):
                copy.wait_send()

        @pl.when(c >= LOOK_PAR)
        def _():
            for copy in pair_send(c):
                copy.wait_send()

    def iteration(t, carry):
        @pl.when(t + LOOK_PAR < chunks)
        def _():
            c = t + LOOK_PAR
            xh_recv(c).wait_recv()
            start(pair_send(c))

        @pl.when(t + LOOK_XH < chunks)
        def _():
            xh_send(t + LOOK_XH).start()

        @pl.when(t + 1 < LOOK_PAR)
        def _():
            wait_recv(own_recv(t + 1))
            wait_recv(par_recv(t + 1))

        @pl.when(jnp.logical_and(t + 1 >= LOOK_PAR, t + 1 < chunks))
        def _():
            wait_recv(pair_recv(t + 1))

        @pl.when(t + 1 < chunks)
        def _():
            start(fwd_send(t + 1))

        @pl.when(t < chunks)
        def _():
            wait_recv(fwd_recv(t))
            multiply(t)
            core_copy(t).start()

        @pl.when(jnp.logical_and(t >= 1, t - 1 < chunks))
        def _():
            c = t - 1
            core_copy(c).wait_recv()
            for a in range(XL):
                prod[c, a, z2, k] = prod[c, a, z2, k] + cr[c, a, z2]
            start(z1_copy(c))

        @pl.when(jnp.logical_and(t >= LAG_Z2, t - LAG_Z2 < chunks))
        def _():
            c = t - LAG_Z2
            wait_recv(z1_copy(c))
            for a in range(XL):
                prod[c, a, zp, k, :, 0:half] = (
                    prod[c, a, zp, k, :, 0:half] + cr[c, a, zp, :, 0:half] + z1p[c, a])
                prod[c, a, zp, k, :, half:] = prod[c, a, zp, k, :, half:] + cr[c, a, zp, :, half:]
                prod[c, a, zm, k, :, 0:half] = prod[c, a, zm, k, :, 0:half] + cr[c, a, zm, :, 0:half]
                prod[c, a, zm, k, :, half:] = (
                    prod[c, a, zm, k, :, half:] + cr[c, a, zm, :, half:] + z1m[c, a])
            start(z2_copy(c))

        @pl.when(jnp.logical_and(t >= LAG_FIN, t - LAG_FIN < chunks))
        def _():
            c = t - LAG_FIN
            wait_recv(z2_copy(c))
            for a in range(XL):
                prod[c, a, z, k] = prod[c, a, z, k] + cr[c, a, z] + z2p[c, a] + z2m[c, a]
            xl_copy(c).start()

        @pl.when(t > LAG_OUT)
        def _():
            drain(t - LAG_OUT - 1)

        @pl.when(t >= LAG_OUT)
        def _():
            c = t - LAG_OUT
            xl_copy(c).wait_recv()
            v = prod[c, xl, z, k] + xb[c]
            out[c] = v
            out_copy(c).start()
            total = jnp.sum(fold_lanes(v * in_center - jnp.abs(v) * in_radius), axis=1, keepdims=True)
            tb[...] += jnp.where(lane8 == row8 + c * 8, jnp.broadcast_to(total, (8, LANES)), 0.0)

        @pl.when(jnp.logical_and(t == 2, n // 2 == s))
        def _():
            shift_recv()
            total = sb[0]
            for j in range(1, NNEUR):
                total = total + sb[j]
            tb[...] += jnp.where(row8 == 0, total + bias16[pl.ds(n, 1), :], 0.0)

        return carry

    lax.fori_loop(0, chunks + LAG_OUT, iteration, 0)

    pb[s] = tb[...]

    def pb_copy(j, src):
        return pltpu.make_async_remote_copy(
            src_ref=pb.at[src], dst_ref=pb.at[src], send_sem=pb_s.at[j], recv_sem=pb_r.at[j],
            device_id=((s + j) % NSPEC, n), device_id_type=MESH)

    for j in range(1, NSPEC):
        pb_copy(j, s).start()
    for j in range(1, NSPEC):
        pb_copy(j, (s + NSPEC - j) % NSPEC).wait_recv()
    bound = pb[0]
    for j in range(1, NSPEC):
        bound = bound + pb[j]
    bound = jnp.broadcast_to(jnp.sum(bound, axis=0, keepdims=True), (8, LANES))
    bb[n] = bound
    lbound[...] = bound[0:1, 0:lbound.shape[1]]

    def bb_copy(j, src):
        return pltpu.make_async_remote_copy(
            src_ref=bb.at[src], dst_ref=bb.at[src], send_sem=bb_s.at[j], recv_sem=bb_r.at[j],
            device_id=(s, (n + j) % NNEUR), device_id_type=MESH)

    for j in range(1, NNEUR):
        bb_copy(j, n).start()

    drain(chunks - 1)
    for h in range(2):
        @pl.when(n != 2 * s + h)
        def _(h=h):
            shs_copy(h).wait_send()

    for j in range(1, NNEUR):
        bb_copy(j, (n + NNEUR - j) % NNEUR).wait_recv()

    row = lax.broadcasted_iota(jnp.int32, (8, 4 * LANES), 0)

    def parts(first):
        v = jnp.concatenate([bb[first + i] for i in range(4)], axis=1)
        p1 = v.astype(BF16).astype(F32)
        p2 = (v - p1).astype(BF16).astype(F32)
        p3 = v - p1 - p2
        return jnp.where(row == 0, p1, jnp.where(row == 1, p2, jnp.where(row == 2, p3, 0.0)))

    for b in range(2):
        lhs = jnp.concatenate([parts(8 * b), parts(8 * b + 4)], axis=0).astype(BF16)
        picked = jnp.dot(lhs, onehot[b], preferred_element_type=F32)
        low_found = jnp.sum(picked[0:8], axis=0, keepdims=True)
        high_found = -jnp.sum(picked[8:16], axis=0, keepdims=True)
        hit = touched[b:b + 1, :] > 0.0
        low0, high0 = plow[b:b + 1, :], phigh[b:b + 1, :]
        new_low = jnp.where(hit, jnp.maximum(low0, low_found), low0)
        new_high = jnp.where(hit, jnp.minimum(high0, high_found), high0)
        rising, falling = jnp.maximum(new_high, 0.0), jnp.maximum(-new_low, 0.0)
        unstable = jnp.logical_and(new_low < 0.0, new_high > 0.0)
        safe = jnp.where(unstable, rising + falling, 1.0)
        slope = jnp.where(new_low >= 0.0, 1.0, jnp.where(new_high <= 0.0, 0.0, rising / safe))
        nslope[b:b + 1, :] = slope
        nshift[b:b + 1, :] = slope * falling

    for j in range(1, NSPEC):
        pb_copy(j, s).wait_send()
    for j in range(1, NNEUR):
        bb_copy(j, n).wait_send()


def per_device(panel, weight, layer_bias, act_center, act_radius, alpha, in_center, in_radius,
               bias_in, spec_neuron, prior_lower, prior_upper):
    own_rows, kdim = panel.shape
    ndim = weight.shape[1]
    hrows = own_rows // 2
    chunks = hrows // 8
    spec_rows = bias_in.shape[0] // NNEUR
    vmem = pl.BlockSpec(memory_space=pltpu.VMEM)
    hbm = pl.BlockSpec(memory_space=pl.ANY)
    half = ndim // 2
    dma = pltpu.SemaphoreType.DMA
    small_in = (layer_bias.reshape(1, kdim), act_center, act_radius, alpha, in_center, in_radius,
                bias_in.reshape(-1, LANES), spec_neuron, prior_lower, prior_upper)
    results = pl.pallas_call(
        kernel,
        out_shape=(
            jax.ShapeDtypeStruct((hrows, ndim), F32),
            jax.ShapeDtypeStruct((1, spec_rows), F32),
            jax.ShapeDtypeStruct((2, kdim), F32),
            jax.ShapeDtypeStruct((2, kdim), F32),
        ),
        in_specs=[hbm] * 12,
        out_specs=(hbm, vmem, vmem, vmem),
        scratch_shapes=[pltpu.VMEM(a.shape, a.dtype) for a in small_in] + [
            pltpu.VMEM((2, hrows, kdim), F32),
            pltpu.VMEM((kdim // W_ROWS, W_ROWS, ndim), F32),
            pltpu.VMEM((kdim, ndim), BF16),
            pltpu.VMEM((kdim, ndim), BF16),
            pltpu.VMEM((chunks, XH, Y, 2, 8, kdim), F32),
            pltpu.VMEM((2 * 16 * NSPEC, kdim), BF16),
            pltpu.VMEM((chunks, XL, Z, 2, 8, ndim), F32),
            pltpu.VMEM((chunks, XL, Z, 8, ndim), F32),
            pltpu.VMEM((chunks, XL, 8, half), F32),
            pltpu.VMEM((chunks, XL, 8, half), F32),
            pltpu.VMEM((chunks, XL, 8, ndim), F32),
            pltpu.VMEM((chunks, XL, 8, ndim), F32),
            pltpu.VMEM((chunks, 8, ndim), F32),
            pltpu.VMEM((2, LANES, LANES), F32),
            pltpu.VMEM((8, LANES), F32),
            pltpu.VMEM((2, 8, LANES), F32),
            pltpu.VMEM((NNEUR, 8, LANES), F32),
            pltpu.VMEM((NSPEC, 8, LANES), F32),
            pltpu.VMEM((NNEUR, 8, LANES), F32),
            pltpu.VMEM((2, 4 * LANES, kdim), BF16),
            pltpu.VMEM((2, kdim), F32),
            pltpu.VMEM((NNEUR, LANES), F32),
            pltpu.VMEM((chunks, 8, ndim), F32),
            dma((11 + kdim // W_ROWS,)), dma((chunks,)),
            dma((chunks, NCOPY)), dma((chunks, NCOPY)),
            dma((2,)), dma((NNEUR,)),
            dma((NSPEC,)), dma((NSPEC,)),
            dma((NNEUR,)), dma((NNEUR,)),
        ],
        compiler_params=pltpu.CompilerParams(
            collective_id=0, has_side_effects=True, vmem_limit_bytes=60 * 1024 * 1024),
        cost_estimate=pl.CostEstimate(
            flops=6 * 8 * own_rows * kdim * ndim, bytes_accessed=4 * kdim * ndim, transcendentals=0),
    )(panel.reshape(2, hrows, kdim), weight, *small_in)
    coef, lbound, nslope, nshift = hand_on(results)
    return coef, lbound.reshape(spec_rows), nslope, nshift


def hand_on(arrays):
    count = len(arrays)
    parts = 6
    step = arrays[0].shape[0] // parts

    def copy_kernel(*refs):
        held = refs[2 * count:3 * count]
        sems_in, sems_out = refs[3 * count:]

        def moves(source, target, sems):
            pairs = [(source[0].at[pl.ds(i * step, step)], target[0].at[pl.ds(i * step, step)])
                     for i in range(parts)]
            pairs += [(source[i], target[i]) for i in range(1, count)]
            return [pltpu.make_async_copy(a, b, sems.at[i]) for i, (a, b) in enumerate(pairs)]

        into, outof = moves(refs[:count], held, sems_in), moves(held, refs[count:2 * count], sems_out)
        for copy in into:
            copy.start()
        for first, second in zip(into, outof):
            first.wait()
            second.start()
        for copy in outof:
            copy.wait()

    hbm = pl.BlockSpec(memory_space=pl.ANY)
    return pl.pallas_call(
        copy_kernel,
        out_shape=tuple(jax.ShapeDtypeStruct(a.shape, a.dtype) for a in arrays),
        in_specs=[hbm] * count,
        out_specs=(hbm,) * count,
        scratch_shapes=[pltpu.VMEM(a.shape, a.dtype) for a in arrays]
        + [pltpu.SemaphoreType.DMA((parts + count,))] * 2,
    )(*arrays)


def solution(mesh):
    in_specs = (
        P("spec", "neuron"),
        P("neuron", "spec"),
        P("neuron"),
        P(None, "neuron"),
        P(None, "neuron"),
        P(None, "neuron"),
        P(None, "spec"),
        P(None, "spec"),
        P(),
        P(),
        P(None, "neuron"),
        P(None, "neuron"),
    )
    out_specs = (P("neuron", "spec"), P("neuron"), P(None, "neuron"), P(None, "neuron"))
    return jax.shard_map(
        per_device, mesh=mesh, in_specs=in_specs, out_specs=out_specs, check_vma=False
    )
```

```python
import functools

import jax
import jax.numpy as jnp
from jax import lax
from jax.experimental import pallas as pl
from jax.experimental.pallas import tpu as pltpu
from jax.sharding import PartitionSpec as P

MESH = pl.DeviceIdType.MESH
F32 = jnp.float32
BF16 = jnp.bfloat16
XH, Y, XL, Z = 2, 4, 2, 4
NSPEC, NNEUR = XH * Y, XL * Z * 2
LANES = 128

(S_XH, S_OWN_P, S_OWN_M, S_PAR_P, S_PAR_M, S_PAIR_P, S_PAIR_M, S_FWD_P, S_FWD_M,
 S_CORE, S_Z1_P, S_Z1_M, S_Z2_P, S_Z2_M, S_XL) = range(15)
NCOPY = 15

LAG_Z2 = 2
LAG_FIN = 4
LAG_OUT = 5
LOOK_XH = 4
LOOK_PAR = 2
TILE_N = 1024
W_ROWS = 256


def fold_lanes(v):
    out = v[:, 0:LANES]
    for g in range(1, v.shape[1] // LANES):
        out = out + v[:, g * LANES:(g + 1) * LANES]
    return out


def rows_to_lanes(t):
    return lax.dot_general(
        jnp.ones((8, LANES), F32), t, (((1,), (1,)), ((), ())),
        precision=lax.Precision.HIGHEST, preferred_element_type=F32)


def kernel(panel, weight, *rest):
    small_in = rest[:10]
    coef = rest[10]
    lbound, nslope, nshift = rest[11:14]
    small = rest[14:24]
    body(panel, weight, small_in, small, coef, lbound, nslope, nshift, *rest[24:])


def body(panel, weight, small_in, small, coef, lbound, nslope, nshift,
           pan, wst, whi, wlo, g, asp, prod, cr, z1p, z1m, z2p, z2m, xb,
           ts, tb, shs, sb, pb, bb, onehot, touched, bias16, out,
           dsem, osem, ssem, rsem, shs_s, shs_r, pb_s, pb_r, bb_s, bb_r):
    chunks = g.shape[0]
    kdim, ndim = whi.shape
    half = ndim // 2
    s = lax.axis_index("spec")
    n = lax.axis_index("neuron")
    xh, y = s // Y, s % Y
    xl, z, k = n // (2 * Z), (n // 2) % Z, n % 2
    yp, ym, y2 = (y + 1) % Y, (y + 3) % Y, (y + 2) % Y
    zp, zm, z2 = (z + 1) % Z, (z + 3) % Z, (z + 2) % Z

    dev_xh = ((1 - xh) * Y + y, n)
    dev_yp, dev_ym = (xh * Y + yp, n), (xh * Y + ym, n)
    dev_core = (s, xl * 2 * Z + z * 2 + (1 - k))
    dev_zp, dev_zm = (s, xl * 2 * Z + zp * 2 + k), (s, xl * 2 * Z + zm * 2 + k)
    dev_xl = (s, (1 - xl) * 2 * Z + z * 2 + k)

    barrier = pltpu.get_barrier_semaphore()
    near = (dev_xh, dev_yp, dev_ym, dev_core, dev_zp, dev_zm, dev_xl)
    for dev in near:
        pl.semaphore_signal(barrier, inc=1, device_id=dev, device_id_type=MESH)

    loads = [pltpu.make_async_copy(a, b, dsem.at[i]) for i, (a, b) in enumerate(zip(small_in, small))]
    load_panel = pltpu.make_async_copy(panel, pan, dsem.at[10])
    for load in loads[:4]:
        load.start()
    load_panel.start()
    for load in loads[4:]:
        load.start()
    pieces = kdim // W_ROWS
    w_loads = [
        pltpu.make_async_copy(weight.at[pl.ds(i * W_ROWS, W_ROWS)], wst.at[i], dsem.at[11 + i])
        for i in range(pieces)]
    for w_load in w_loads:
        w_load.start()
    lbias, ac, ar, al, ic, ir, bias, names, plow, phigh = small

    for load in loads[:4]:
        load.wait()

    def pick(ref, i):
        return jnp.where(i == 0, ref[0:1, :], ref[1:2, :])

    center, radius = pick(ac, xh), pick(ar, xh)
    act_low, act_high = center - radius, center + radius
    upper, lower = jnp.maximum(act_high, 0.0), jnp.maximum(-act_low, 0.0)
    up_slope = upper / (upper + lower)
    up_shift = up_slope * lower
    low_slope = jnp.where(act_low >= 0.0, 1.0, jnp.where(act_high <= 0.0, 0.0, pick(al, xh)))
    lb = lbias[...]
    ts[...] = jnp.zeros_like(ts)
    tb[...] = jnp.zeros_like(tb)
    load_panel.wait()

    def relax(c, carry):
        for h in range(2):
            p = pan[h, pl.ds(pl.multiple_of(c * 8, 8), 8), :]
            neg = jnp.minimum(p, 0.0)
            rel = low_slope * jnp.maximum(p, 0.0) + up_slope * neg
            g[c, xh, y, h] = rel
            ts[h, pl.ds(pl.multiple_of(c * 8, 8), 8), :] = fold_lanes(rel * lb + neg * up_shift)
        return carry

    first = min(LOOK_PAR, chunks)
    lax.fori_loop(0, first, relax, 0)
    pl.semaphore_wait(barrier, len(near))

    def rc(src, dst, kind, c, dev):
        return pltpu.make_async_remote_copy(
            src_ref=src, dst_ref=dst, send_sem=ssem.at[kind], recv_sem=rsem.at[c, kind],
            device_id=dev, device_id_type=MESH)

    def block_copy(kind, c, bx, by, dev):
        return rc(g.at[c, bx, by], g.at[c, bx, by], kind, c, dev)

    def pair_copy(kind, c, by, dev):
        return rc(g.at[c, :, by], g.at[c, :, by], kind, c, dev)

    def half_copy(kind, c, by, h, dev):
        return rc(g.at[c, :, by, h], g.at[c, :, by, h], kind, c, dev)

    def xh_send(c): return block_copy(S_XH, c, xh, y, dev_xh)
    def xh_recv(c): return block_copy(S_XH, c, 1 - xh, y, dev_xh)

    def own_send(c):
        return [block_copy(S_OWN_P, c, xh, y, dev_yp), block_copy(S_OWN_M, c, xh, y, dev_ym)]

    def own_recv(c):
        return [block_copy(S_OWN_P, c, xh, ym, dev_yp), block_copy(S_OWN_M, c, xh, yp, dev_ym)]

    def par_send(c):
        return [block_copy(S_PAR_P, c, 1 - xh, y, dev_yp), block_copy(S_PAR_M, c, 1 - xh, y, dev_ym)]

    def par_recv(c):
        return [block_copy(S_PAR_P, c, 1 - xh, ym, dev_yp), block_copy(S_PAR_M, c, 1 - xh, yp, dev_ym)]

    def pair_send(c):
        return [pair_copy(S_PAIR_P, c, y, dev_yp), pair_copy(S_PAIR_M, c, y, dev_ym)]

    def pair_recv(c):
        return [pair_copy(S_PAIR_P, c, ym, dev_yp), pair_copy(S_PAIR_M, c, yp, dev_ym)]

    def fwd_send(c):
        return [half_copy(S_FWD_P, c, ym, 0, dev_yp), half_copy(S_FWD_M, c, yp, 1, dev_ym)]

    def fwd_recv(c):
        return [half_copy(S_FWD_P, c, y2, 0, dev_yp), half_copy(S_FWD_M, c, y2, 1, dev_ym)]

    def core_copy(c):
        return rc(prod.at[c, :, :, 1 - k], cr.at[c], S_CORE, c, dev_core)

    def z1_copy(c):
        return [rc(prod.at[c, :, z2, k, :, pl.ds(0, half)], z1p.at[c], S_Z1_P, c, dev_zp),
                rc(prod.at[c, :, z2, k, :, pl.ds(half, half)], z1m.at[c], S_Z1_M, c, dev_zm)]

    def z2_copy(c):
        return [rc(prod.at[c, :, zp, k], z2p.at[c], S_Z2_P, c, dev_zp),
                rc(prod.at[c, :, zm, k], z2m.at[c], S_Z2_M, c, dev_zm)]

    def xl_copy(c):
        return rc(prod.at[c, 1 - xl, z, k], xb.at[c], S_XL, c, dev_xl)

    def out_copy(c):
        return pltpu.make_async_copy(
            out.at[pl.ds(pl.multiple_of(c * 8, 8), 8)], coef.at[pl.ds(pl.multiple_of(c * 8, 8), 8)], osem.at[0])

    def start(copies):
        for copy in copies:
            copy.start()

    def wait_recv(copies):
        for copy in copies:
            copy.wait_recv()

    for c in range(first):
        xh_send(c).start()
        start(own_send(c))
    lax.fori_loop(first, chunks, relax, 0)
    for c in range(LOOK_PAR, min(LOOK_XH, chunks)):
        xh_send(c).start()

    for h in range(2):
        shs[h] = rows_to_lanes(ts[h])

    def shs_copy(h):
        return pltpu.make_async_remote_copy(
            src_ref=shs.at[h], dst_ref=sb.at[n], send_sem=shs_s.at[h], recv_sem=shs_r.at[n],
            device_id=(s, 2 * s + h), device_id_type=MESH)

    def split_piece(i):
        def body(r, carry):
            w = wst[i, pl.ds(pl.multiple_of(r * 16, 16), 16), :]
            hi = w.astype(BF16)
            rows = pl.ds(pl.multiple_of(i * W_ROWS + r * 16, 16), 16)
            whi[rows, :] = hi
            wlo[rows, :] = (w - hi.astype(F32)).astype(BF16)
            return carry
        w_loads[i].wait()
        lax.fori_loop(0, W_ROWS // 16, body, 0)

    split_piece(0)
    for c in range(min(LOOK_PAR, chunks)):
        xh_recv(c).wait_recv()
        start(par_send(c))
        split_piece(1 + c)
    wait_recv(own_recv(0))
    wait_recv(par_recv(0))
    start(fwd_send(0))
    for i in range(1 + min(LOOK_PAR, chunks), pieces):
        split_piece(i)

    for load in loads[4:]:
        load.wait()

    def row_piece(v, first, count):
        at = first // LANES * LANES
        if first % LANES == 0:
            return v[:, at:at + LANES]
        width = min(2 * LANES, v.shape[1] - at)
        return pltpu.roll(v[:, at:at + width], width - first % LANES, 1)[:, 0:LANES]

    spec_rows = lbound.shape[1]
    lane = lax.broadcasted_iota(jnp.int32, (1, LANES), 1)
    bias_row = jnp.concatenate([bias[i:i + 1, :] for i in range(bias.shape[0])], axis=1)
    for j in range(NNEUR):
        piece = row_piece(bias_row, j * spec_rows, spec_rows)
        bias16[j:j + 1, :] = jnp.where(lane < spec_rows, piece, 0.0)
    def shift_recv():
        for j in range(1, NNEUR):
            other = (n + j) % NNEUR
            pltpu.make_async_remote_copy(
                src_ref=sb.at[other], dst_ref=sb.at[other], send_sem=shs_s.at[0],
                recv_sem=shs_r.at[other], device_id=(s, other), device_id_type=MESH).wait_recv()

    in_center, in_radius = pick(ic, xl), pick(ir, xl)
    row8 = lax.broadcasted_iota(jnp.int32, (8, LANES), 0)
    lane8 = lax.broadcasted_iota(jnp.int32, (8, LANES), 1)

    def multiply(c, part):
        if part == 0:
            a = g[c].reshape(16 * NSPEC, kdim)
            hi = a.astype(BF16)
            asp[0:16 * NSPEC, :] = hi
            asp[16 * NSPEC:, :] = (a - hi.astype(F32)).astype(BF16)

        def tile(j, carry):
            cols = pl.ds(pl.multiple_of(j * TILE_N, TILE_N), TILE_N)
            both = jnp.dot(asp[...], whi[:, cols], preferred_element_type=F32)
            rest = jnp.dot(asp[0:16 * NSPEC, :], wlo[:, cols], preferred_element_type=F32)
            res = both[0:16 * NSPEC] + both[16 * NSPEC:] + rest
            prod[c, :, :, :, :, cols] = res.reshape(XL, Z, 2, 8, TILE_N)
            return carry

        half_tiles = ndim // TILE_N // 2
        lax.fori_loop(part * half_tiles, (part + 1) * half_tiles, tile, 0)

    def stage(cond, body):
        pl.when(cond)(body)

    def find_columns():
        columns = (n * kdim).astype(F32)
        for b in range(2):
            for q in range(4):
                row = row_piece(names[b:b + 1, :].astype(F32), q * spec_rows, spec_rows)
                row = jnp.broadcast_to(jnp.where(lane < spec_rows, row, -1.0), (LANES, LANES))
                target = row.T - columns
                for t in range(kdim // LANES):
                    ids = lax.broadcasted_iota(jnp.int32, (LANES, LANES), 1).astype(F32) + float(t * LANES)
                    hit = jnp.where(target == ids, 1.0, 0.0)
                    onehot[b, q * LANES:(q + 1) * LANES, t * LANES:(t + 1) * LANES] = hit.astype(BF16)
            total = jnp.dot(jnp.ones((16, 4 * LANES), BF16), onehot[b], preferred_element_type=F32)
            touched[b:b + 1, :] = total[0:1, :]

    def iteration(t, carry):
        @pl.when(t + LOOK_PAR < chunks)
        def _():
            c = t + LOOK_PAR
            xh_recv(c).wait_recv()
            start(pair_send(c))

        @pl.when(t + LOOK_XH < chunks)
        def _():
            xh_send(t + LOOK_XH).start()

        @pl.when(t + 1 < LOOK_PAR)
        def _():
            wait_recv(own_recv(t + 1))
            wait_recv(par_recv(t + 1))

        @pl.when(jnp.logical_and(t + 1 >= LOOK_PAR, t + 1 < chunks))
        def _():
            wait_recv(pair_recv(t + 1))

        @pl.when(t + 1 < chunks)
        def _():
            start(fwd_send(t + 1))

        @pl.when(t < chunks)
        def _():
            wait_recv(fwd_recv(t))
            multiply(t, 0)

        @pl.when(jnp.logical_and(t >= 1, t - 1 < chunks))
        def _():
            c = t - 1
            core_copy(c).wait_recv()
            for a in range(XL):
                prod[c, a, z2, k] = prod[c, a, z2, k] + cr[c, a, z2]
            start(z1_copy(c))

        @pl.when(t < chunks)
        def _():
            multiply(t, 1)
            core_copy(t).start()

        @pl.when(jnp.logical_and(t >= LAG_Z2, t - LAG_Z2 < chunks))
        def _():
            c = t - LAG_Z2
            wait_recv(z1_copy(c))
            for a in range(XL):
                prod[c, a, zp, k, :, 0:half] = (
                    prod[c, a, zp, k, :, 0:half] + cr[c, a, zp, :, 0:half] + z1p[c, a])
                prod[c, a, zp, k, :, half:] = prod[c, a, zp, k, :, half:] + cr[c, a, zp, :, half:]
                prod[c, a, zm, k, :, 0:half] = prod[c, a, zm, k, :, 0:half] + cr[c, a, zm, :, 0:half]
                prod[c, a, zm, k, :, half:] = (
                    prod[c, a, zm, k, :, half:] + cr[c, a, zm, :, half:] + z1m[c, a])
            start(z2_copy(c))

        @pl.when(t == chunks + LAG_Z2 - 1)
        def _():
            find_columns()

        @pl.when(jnp.logical_and(t >= LAG_FIN, t - LAG_FIN < chunks))
        def _():
            c = t - LAG_FIN
            wait_recv(z2_copy(c))
            for a in range(XL):
                prod[c, a, z, k] = prod[c, a, z, k] + cr[c, a, z] + z2p[c, a] + z2m[c, a]
            xl_copy(c).start()

        @pl.when(t >= LAG_OUT)
        def _():
            c = t - LAG_OUT
            xl_copy(c).wait_recv()
            v = prod[c, xl, z, k] + xb[c]
            out[pl.ds(pl.multiple_of(c * 8, 8), 8), :] = v
            out_copy(c).start()
            total = jnp.sum(fold_lanes(v * in_center - jnp.abs(v) * in_radius), axis=1, keepdims=True)
            tb[...] += jnp.where(lane8 == row8 + c * 8, jnp.broadcast_to(total, (8, LANES)), 0.0)

        @pl.when(t == LAG_OUT + 1)
        def _():
            for h in range(2):
                @pl.when(n != 2 * s + h)
                def _(h=h):
                    shs_copy(h).start()

                @pl.when(n == 2 * s + h)
                def _(h=h):
                    sb[n] = shs[h]

        @pl.when(jnp.logical_and(t == LAG_OUT + 4, n // 2 == s))
        def _():
            shift_recv()
            total = sb[0]
            for j in range(1, NNEUR):
                total = total + sb[j]
            tb[...] += jnp.where(row8 == 0, total + bias16[pl.ds(n, 1), :], 0.0)

        return carry

    lax.fori_loop(0, chunks + LAG_OUT, iteration, 0)

    pb[s] = tb[...]

    def pb_copy(j, src):
        return pltpu.make_async_remote_copy(
            src_ref=pb.at[src], dst_ref=pb.at[src], send_sem=pb_s.at[j], recv_sem=pb_r.at[j],
            device_id=((s + j) % NSPEC, n), device_id_type=MESH)

    for j in range(1, NSPEC):
        pb_copy(j, s).start()
    for j in range(1, NSPEC):
        pb_copy(j, (s + NSPEC - j) % NSPEC).wait_recv()
    bound = pb[0]
    for j in range(1, NSPEC):
        bound = bound + pb[j]
    bound = jnp.broadcast_to(jnp.sum(bound, axis=0, keepdims=True), (8, LANES))
    bb[n] = bound
    lbound[...] = bound[0:1, 0:lbound.shape[1]]

    def bb_copy(j, src):
        return pltpu.make_async_remote_copy(
            src_ref=bb.at[src], dst_ref=bb.at[src], send_sem=bb_s.at[j], recv_sem=bb_r.at[j],
            device_id=(s, (n + j) % NNEUR), device_id_type=MESH)

    for j in range(1, NNEUR):
        bb_copy(j, n).start()

    def sent(src, kind):
        pltpu.make_async_remote_copy(
            src_ref=src, dst_ref=src, send_sem=ssem.at[kind], recv_sem=rsem.at[0, kind],
            device_id=dev_core, device_id_type=MESH).wait_send()

    rest = pl.ds(LOOK_PAR, chunks - LOOK_PAR)
    sent(g.at[:, xh, y], S_XH)
    for kind in (S_OWN_P, S_OWN_M, S_PAR_P, S_PAR_M):
        sent(g.at[pl.ds(0, LOOK_PAR), xh, y], kind)
    for kind in (S_PAIR_P, S_PAIR_M):
        sent(g.at[rest, :, y], kind)
    for kind in (S_FWD_P, S_FWD_M):
        sent(g.at[:, :, y, 0], kind)
    sent(prod.at[:, :, :, 1 - k], S_CORE)
    for kind in (S_Z1_P, S_Z1_M):
        sent(prod.at[:, :, z2, k, :, pl.ds(0, half)], kind)
    for kind in (S_Z2_P, S_Z2_M):
        sent(prod.at[:, :, z, k], kind)
    sent(prod.at[:, 1 - xl, z, k], S_XL)
    pltpu.make_async_copy(out, coef, osem.at[0]).wait()
    for h in range(2):
        @pl.when(n != 2 * s + h)
        def _(h=h):
            shs_copy(h).wait_send()

    for j in range(1, NNEUR):
        bb_copy(j, (n + NNEUR - j) % NNEUR).wait_recv()

    row = lax.broadcasted_iota(jnp.int32, (8, 4 * LANES), 0)

    def parts(first):
        v = jnp.concatenate([bb[first + i] for i in range(4)], axis=1)
        p1 = v.astype(BF16).astype(F32)
        p2 = (v - p1).astype(BF16).astype(F32)
        p3 = v - p1 - p2
        return jnp.where(row == 0, p1, jnp.where(row == 1, p2, jnp.where(row == 2, p3, 0.0)))

    for b in range(2):
        lhs = jnp.concatenate([parts(8 * b), parts(8 * b + 4)], axis=0).astype(BF16)
        picked = jnp.dot(lhs, onehot[b], preferred_element_type=F32)
        low_found = jnp.sum(picked[0:8], axis=0, keepdims=True)
        high_found = -jnp.sum(picked[8:16], axis=0, keepdims=True)
        hit = touched[b:b + 1, :] > 0.0
        low0, high0 = plow[b:b + 1, :], phigh[b:b + 1, :]
        new_low = jnp.where(hit, jnp.maximum(low0, low_found), low0)
        new_high = jnp.where(hit, jnp.minimum(high0, high_found), high0)
        rising, falling = jnp.maximum(new_high, 0.0), jnp.maximum(-new_low, 0.0)
        unstable = jnp.logical_and(new_low < 0.0, new_high > 0.0)
        safe = jnp.where(unstable, rising + falling, 1.0)
        slope = jnp.where(new_low >= 0.0, 1.0, jnp.where(new_high <= 0.0, 0.0, rising / safe))
        nslope[b:b + 1, :] = slope
        nshift[b:b + 1, :] = slope * falling

    for j in range(1, NSPEC):
        pb_copy(j, s).wait_send()
    for j in range(1, NNEUR):
        bb_copy(j, n).wait_send()


def per_device(panel, weight, layer_bias, act_center, act_radius, alpha, in_center, in_radius,
               bias_in, spec_neuron, prior_lower, prior_upper):
    own_rows, kdim = panel.shape
    ndim = weight.shape[1]
    hrows = own_rows // 2
    chunks = hrows // 8
    spec_rows = bias_in.shape[0] // NNEUR
    vmem = pl.BlockSpec(memory_space=pltpu.VMEM)
    hbm = pl.BlockSpec(memory_space=pl.ANY)
    half = ndim // 2
    dma = pltpu.SemaphoreType.DMA
    small_in = (layer_bias.reshape(1, kdim), act_center, act_radius, alpha, in_center, in_radius,
                bias_in.reshape(-1, LANES), spec_neuron, prior_lower, prior_upper)
    results = pl.pallas_call(
        kernel,
        out_shape=(
            jax.ShapeDtypeStruct((hrows, ndim), F32),
            jax.ShapeDtypeStruct((1, spec_rows), F32),
            jax.ShapeDtypeStruct((2, kdim), F32),
            jax.ShapeDtypeStruct((2, kdim), F32),
        ),
        in_specs=[hbm] * 12,
        out_specs=(hbm, vmem, vmem, vmem),
        scratch_shapes=[pltpu.VMEM(a.shape, a.dtype) for a in small_in] + [
            pltpu.VMEM((2, hrows, kdim), F32),
            pltpu.VMEM((kdim // W_ROWS, W_ROWS, ndim), F32),
            pltpu.VMEM((kdim, ndim), BF16),
            pltpu.VMEM((kdim, ndim), BF16),
            pltpu.VMEM((chunks, XH, Y, 2, 8, kdim), F32),
            pltpu.VMEM((2 * 16 * NSPEC, kdim), BF16),
            pltpu.VMEM((chunks, XL, Z, 2, 8, ndim), F32),
            pltpu.VMEM((chunks, XL, Z, 8, ndim), F32),
            pltpu.VMEM((chunks, XL, 8, half), F32),
            pltpu.VMEM((chunks, XL, 8, half), F32),
            pltpu.VMEM((chunks, XL, 8, ndim), F32),
            pltpu.VMEM((chunks, XL, 8, ndim), F32),
            pltpu.VMEM((chunks, 8, ndim), F32),
            pltpu.VMEM((2, LANES, LANES), F32),
            pltpu.VMEM((8, LANES), F32),
            pltpu.VMEM((2, 8, LANES), F32),
            pltpu.VMEM((NNEUR, 8, LANES), F32),
            pltpu.VMEM((NSPEC, 8, LANES), F32),
            pltpu.VMEM((NNEUR, 8, LANES), F32),
            pltpu.VMEM((2, 4 * LANES, kdim), BF16),
            pltpu.VMEM((2, kdim), F32),
            pltpu.VMEM((NNEUR, LANES), F32),
            pltpu.VMEM((hrows, ndim), F32),
            dma((11 + kdim // W_ROWS,)), dma((1,)),
            dma((NCOPY,)), dma((chunks, NCOPY)),
            dma((2,)), dma((NNEUR,)),
            dma((NSPEC,)), dma((NSPEC,)),
            dma((NNEUR,)), dma((NNEUR,)),
        ],
        compiler_params=pltpu.CompilerParams(
            collective_id=0, has_side_effects=True, vmem_limit_bytes=60 * 1024 * 1024),
        cost_estimate=pl.CostEstimate(
            flops=6 * 8 * own_rows * kdim * ndim, bytes_accessed=4 * kdim * ndim, transcendentals=0),
    )(panel.reshape(2, hrows, kdim), weight, *small_in)
    coef, lbound, nslope, nshift = hand_on(results)
    return coef, lbound.reshape(spec_rows), nslope, nshift


def hand_on(arrays):
    count = len(arrays)
    parts = 6
    step = arrays[0].shape[0] // parts

    def copy_kernel(*refs):
        held = refs[2 * count:3 * count]
        sems_in, sems_out = refs[3 * count:]

        def moves(source, target, sems):
            pairs = [(source[0].at[pl.ds(i * step, step)], target[0].at[pl.ds(i * step, step)])
                     for i in range(parts)]
            pairs += [(source[i], target[i]) for i in range(1, count)]
            return [pltpu.make_async_copy(a, b, sems.at[i]) for i, (a, b) in enumerate(pairs)]

        into, outof = moves(refs[:count], held, sems_in), moves(held, refs[count:2 * count], sems_out)
        for copy in into:
            copy.start()
        for first, second in zip(into, outof):
            first.wait()
            second.start()
        for copy in outof:
            copy.wait()

    hbm = pl.BlockSpec(memory_space=pl.ANY)
    return pl.pallas_call(
        copy_kernel,
        out_shape=tuple(jax.ShapeDtypeStruct(a.shape, a.dtype) for a in arrays),
        in_specs=[hbm] * count,
        out_specs=(hbm,) * count,
        scratch_shapes=[pltpu.VMEM(a.shape, a.dtype) for a in arrays]
        + [pltpu.SemaphoreType.DMA((parts + count,))] * 2,
    )(*arrays)


def solution(mesh):
    in_specs = (
        P("spec", "neuron"),
        P("neuron", "spec"),
        P("neuron"),
        P(None, "neuron"),
        P(None, "neuron"),
        P(None, "neuron"),
        P(None, "spec"),
        P(None, "spec"),
        P(),
        P(),
        P(None, "neuron"),
        P(None, "neuron"),
    )
    out_specs = (P("neuron", "spec"), P("neuron"), P(None, "neuron"), P(None, "neuron"))
    return jax.shard_map(
        per_device, mesh=mesh, in_specs=in_specs, out_specs=out_specs, check_vma=False
    )
```

```python
import functools

import jax
import jax.numpy as jnp
from jax import lax
from jax.experimental import pallas as pl
from jax.experimental.pallas import tpu as pltpu
from jax.sharding import PartitionSpec as P

MESH = pl.DeviceIdType.MESH
F32 = jnp.float32
BF16 = jnp.bfloat16
XH, Y, XL, Z = 2, 4, 2, 4
NSPEC, NNEUR = XH * Y, XL * Z * 2
LANES = 128

(S_XH, S_OWN_P, S_OWN_M, S_PAR_P, S_PAR_M, S_PAIR_P, S_PAIR_M, S_FWD_P, S_FWD_M,
 S_CORE, S_Z1_P, S_Z1_M, S_Z2_P, S_Z2_M, S_XL) = range(15)
NCOPY = 15

LAG_Z2 = 2
LAG_FIN = 4
LAG_OUT = 5
LOOK_XH = 4
LOOK_PAR = 2
TILE_N = 1024
W_ROWS = 256


def fold_lanes(v):
    out = v[:, 0:LANES]
    for g in range(1, v.shape[1] // LANES):
        out = out + v[:, g * LANES:(g + 1) * LANES]
    return out


def rows_to_lanes(t):
    return lax.dot_general(
        jnp.ones((8, LANES), F32), t, (((1,), (1,)), ((), ())),
        precision=lax.Precision.HIGHEST, preferred_element_type=F32)


def kernel(panel, weight, *rest):
    small_in = rest[:10]
    coef = rest[10]
    lbound, nslope, nshift = rest[11:14]
    small = rest[14:24]
    body(panel, weight, small_in, small, coef, lbound, nslope, nshift, *rest[24:])


def body(panel, weight, small_in, small, coef, lbound, nslope, nshift,
           pan, wst, whi, wlo, g, asp, prod, cr, z1p, z1m, z2p, z2m, xb,
           ts, tb, shs, sb, pb, bb, onehot, touched, bias16, out,
           dsem, osem, ssem, rsem, shs_s, shs_r, pb_s, pb_r, bb_s, bb_r):
    chunks = g.shape[0]
    kdim, ndim = whi.shape
    half = ndim // 2
    s = lax.axis_index("spec")
    n = lax.axis_index("neuron")
    xh, y = s // Y, s % Y
    xl, z, k = n // (2 * Z), (n // 2) % Z, n % 2
    yp, ym, y2 = (y + 1) % Y, (y + 3) % Y, (y + 2) % Y
    zp, zm, z2 = (z + 1) % Z, (z + 3) % Z, (z + 2) % Z

    dev_xh = ((1 - xh) * Y + y, n)
    dev_yp, dev_ym = (xh * Y + yp, n), (xh * Y + ym, n)
    dev_core = (s, xl * 2 * Z + z * 2 + (1 - k))
    dev_zp, dev_zm = (s, xl * 2 * Z + zp * 2 + k), (s, xl * 2 * Z + zm * 2 + k)
    dev_xl = (s, (1 - xl) * 2 * Z + z * 2 + k)

    barrier = pltpu.get_barrier_semaphore()
    near = (dev_xh, dev_yp, dev_ym, dev_core, dev_zp, dev_zm, dev_xl)
    for dev in near:
        pl.semaphore_signal(barrier, inc=1, device_id=dev, device_id_type=MESH)

    loads = [pltpu.make_async_copy(a, b, dsem.at[i]) for i, (a, b) in enumerate(zip(small_in, small))]
    load_panel = pltpu.make_async_copy(panel, pan, dsem.at[10])
    for load in loads[:4]:
        load.start()
    load_panel.start()
    for load in loads[4:]:
        load.start()
    pieces = kdim // W_ROWS
    w_loads = [
        pltpu.make_async_copy(weight.at[pl.ds(i * W_ROWS, W_ROWS)], wst.at[i], dsem.at[11 + i])
        for i in range(pieces)]
    for w_load in w_loads:
        w_load.start()
    lbias, ac, ar, al, ic, ir, bias, names, plow, phigh = small

    for load in loads[:4]:
        load.wait()

    def pick(ref, i):
        return jnp.where(i == 0, ref[0:1, :], ref[1:2, :])

    center, radius = pick(ac, xh), pick(ar, xh)
    act_low, act_high = center - radius, center + radius
    upper, lower = jnp.maximum(act_high, 0.0), jnp.maximum(-act_low, 0.0)
    up_slope = upper / (upper + lower)
    up_shift = up_slope * lower
    low_slope = jnp.where(act_low >= 0.0, 1.0, jnp.where(act_high <= 0.0, 0.0, pick(al, xh)))
    lb = lbias[...]
    ts[...] = jnp.zeros_like(ts)
    tb[...] = jnp.zeros_like(tb)
    load_panel.wait()

    def relax(c, carry):
        for h in range(2):
            p = pan[h, pl.ds(pl.multiple_of(c * 8, 8), 8), :]
            neg = jnp.minimum(p, 0.0)
            rel = low_slope * jnp.maximum(p, 0.0) + up_slope * neg
            g[c, xh, y, h] = rel
            ts[h, pl.ds(pl.multiple_of(c * 8, 8), 8), :] = fold_lanes(rel * lb + neg * up_shift)
        return carry

    first = min(LOOK_PAR, chunks)
    lax.fori_loop(0, first, relax, 0)
    pl.semaphore_wait(barrier, len(near))

    def rc(src, dst, kind, c, dev):
        return pltpu.make_async_remote_copy(
            src_ref=src, dst_ref=dst, send_sem=ssem.at[kind], recv_sem=rsem.at[c, kind],
            device_id=dev, device_id_type=MESH)

    def block_copy(kind, c, bx, by, dev):
        return rc(g.at[c, bx, by], g.at[c, bx, by], kind, c, dev)

    def pair_copy(kind, c, by, dev):
        return rc(g.at[c, :, by], g.at[c, :, by], kind, c, dev)

    def half_copy(kind, c, by, h, dev):
        return rc(g.at[c, :, by, h], g.at[c, :, by, h], kind, c, dev)

    def xh_send(c): return block_copy(S_XH, c, xh, y, dev_xh)
    def xh_recv(c): return block_copy(S_XH, c, 1 - xh, y, dev_xh)

    def own_send(c):
        return [block_copy(S_OWN_P, c, xh, y, dev_yp), block_copy(S_OWN_M, c, xh, y, dev_ym)]

    def own_recv(c):
        return [block_copy(S_OWN_P, c, xh, ym, dev_yp), block_copy(S_OWN_M, c, xh, yp, dev_ym)]

    def par_send(c):
        return [block_copy(S_PAR_P, c, 1 - xh, y, dev_yp), block_copy(S_PAR_M, c, 1 - xh, y, dev_ym)]

    def par_recv(c):
        return [block_copy(S_PAR_P, c, 1 - xh, ym, dev_yp), block_copy(S_PAR_M, c, 1 - xh, yp, dev_ym)]

    def pair_send(c):
        return [pair_copy(S_PAIR_P, c, y, dev_yp), pair_copy(S_PAIR_M, c, y, dev_ym)]

    def pair_recv(c):
        return [pair_copy(S_PAIR_P, c, ym, dev_yp), pair_copy(S_PAIR_M, c, yp, dev_ym)]

    def fwd_send(c):
        return [half_copy(S_FWD_P, c, ym, 0, dev_yp), half_copy(S_FWD_M, c, yp, 1, dev_ym)]

    def fwd_recv(c):
        return [half_copy(S_FWD_P, c, y2, 0, dev_yp), half_copy(S_FWD_M, c, y2, 1, dev_ym)]

    def core_copy(c):
        return rc(prod.at[c, :, :, 1 - k], cr.at[c], S_CORE, c, dev_core)

    def z1_copy(c):
        return [rc(prod.at[c, :, z2, k, :, pl.ds(0, half)], z1p.at[c], S_Z1_P, c, dev_zp),
                rc(prod.at[c, :, z2, k, :, pl.ds(half, half)], z1m.at[c], S_Z1_M, c, dev_zm)]

    def z2_copy(c):
        return [rc(prod.at[c, :, zp, k], z2p.at[c], S_Z2_P, c, dev_zp),
                rc(prod.at[c, :, zm, k], z2m.at[c], S_Z2_M, c, dev_zm)]

    def xl_copy(c):
        return rc(prod.at[c, 1 - xl, z, k], xb.at[c], S_XL, c, dev_xl)

    def out_copy(c):
        return pltpu.make_async_copy(
            out.at[pl.ds(pl.multiple_of(c * 8, 8), 8)], coef.at[pl.ds(pl.multiple_of(c * 8, 8), 8)], osem.at[0])

    def start(copies):
        for copy in copies:
            copy.start()

    def wait_recv(copies):
        for copy in copies:
            copy.wait_recv()

    for c in range(first):
        xh_send(c).start()
        start(own_send(c))
    lax.fori_loop(first, chunks, relax, 0)
    for c in range(LOOK_PAR, min(LOOK_XH, chunks)):
        xh_send(c).start()

    for h in range(2):
        shs[h] = rows_to_lanes(ts[h])

    def shs_copy(h):
        return pltpu.make_async_remote_copy(
            src_ref=shs.at[h], dst_ref=sb.at[n], send_sem=shs_s.at[h], recv_sem=shs_r.at[n],
            device_id=(s, 2 * s + h), device_id_type=MESH)

    def split_piece(i):
        def body(r, carry):
            w = wst[i, pl.ds(pl.multiple_of(r * 16, 16), 16), :]
            hi = w.astype(BF16)
            rows = pl.ds(pl.multiple_of(i * W_ROWS + r * 16, 16), 16)
            whi[rows, :] = hi
            wlo[rows, :] = (w - hi.astype(F32)).astype(BF16)
            return carry
        w_loads[i].wait()
        lax.fori_loop(0, W_ROWS // 16, body, 0)

    split_piece(0)
    for c in range(min(LOOK_PAR, chunks)):
        xh_recv(c).wait_recv()
        start(par_send(c))
        split_piece(1 + c)
    wait_recv(own_recv(0))
    wait_recv(par_recv(0))
    start(fwd_send(0))
    for i in range(1 + min(LOOK_PAR, chunks), pieces):
        split_piece(i)

    for load in loads[4:]:
        load.wait()

    def row_piece(v, first, count):
        at = first // LANES * LANES
        if first % LANES == 0:
            return v[:, at:at + LANES]
        width = min(2 * LANES, v.shape[1] - at)
        return pltpu.roll(v[:, at:at + width], width - first % LANES, 1)[:, 0:LANES]

    spec_rows = lbound.shape[1]
    lane = lax.broadcasted_iota(jnp.int32, (1, LANES), 1)
    bias_row = jnp.concatenate([bias[i:i + 1, :] for i in range(bias.shape[0])], axis=1)
    for j in range(NNEUR):
        piece = row_piece(bias_row, j * spec_rows, spec_rows)
        bias16[j:j + 1, :] = jnp.where(lane < spec_rows, piece, 0.0)
    def shift_recv():
        for j in range(1, NNEUR):
            other = (n + j) % NNEUR
            pltpu.make_async_remote_copy(
                src_ref=sb.at[other], dst_ref=sb.at[other], send_sem=shs_s.at[0],
                recv_sem=shs_r.at[other], device_id=(s, other), device_id_type=MESH).wait_recv()

    in_center, in_radius = pick(ic, xl), pick(ir, xl)
    row8 = lax.broadcasted_iota(jnp.int32, (8, LANES), 0)
    lane8 = lax.broadcasted_iota(jnp.int32, (8, LANES), 1)

    def multiply(c, part):
        if part == 0:
            a = g[c].reshape(16 * NSPEC, kdim)
            hi = a.astype(BF16)
            asp[0:16 * NSPEC, :] = hi
            asp[16 * NSPEC:, :] = (a - hi.astype(F32)).astype(BF16)

        def tile(j, carry):
            cols = pl.ds(j * TILE_N, TILE_N)
            both = jnp.dot(asp[...], whi[:, cols], preferred_element_type=F32)
            rest = jnp.dot(asp[0:16 * NSPEC, :], wlo[:, cols], preferred_element_type=F32)
            res = both[0:16 * NSPEC] + both[16 * NSPEC:] + rest
            prod[c, :, :, :, :, cols] = res.reshape(XL, Z, 2, 8, TILE_N)
            return carry

        tile(part, 0)

    def stage(cond, body):
        pl.when(cond)(body)

    def find_columns():
        columns = (n * kdim).astype(F32)
        for b in range(2):
            for q in range(4):
                row = row_piece(names[b:b + 1, :].astype(F32), q * spec_rows, spec_rows)
                row = jnp.broadcast_to(jnp.where(lane < spec_rows, row, -1.0), (LANES, LANES))
                target = row.T - columns
                for t in range(kdim // LANES):
                    ids = lax.broadcasted_iota(jnp.int32, (LANES, LANES), 1).astype(F32) + float(t * LANES)
                    hit = jnp.where(target == ids, 1.0, 0.0)
                    onehot[b, q * LANES:(q + 1) * LANES, t * LANES:(t + 1) * LANES] = hit.astype(BF16)
            total = jnp.dot(jnp.ones((16, 4 * LANES), BF16), onehot[b], preferred_element_type=F32)
            touched[b:b + 1, :] = total[0:1, :]

    def iteration(t, carry):
        @pl.when(t + LOOK_PAR < chunks)
        def _():
            c = t + LOOK_PAR
            xh_recv(c).wait_recv()
            start(pair_send(c))

        @pl.when(t + LOOK_XH < chunks)
        def _():
            xh_send(t + LOOK_XH).start()

        @pl.when(t + 1 < LOOK_PAR)
        def _():
            wait_recv(own_recv(t + 1))
            wait_recv(par_recv(t + 1))

        @pl.when(jnp.logical_and(t + 1 >= LOOK_PAR, t + 1 < chunks))
        def _():
            wait_recv(pair_recv(t + 1))

        @pl.when(t + 1 < chunks)
        def _():
            start(fwd_send(t + 1))

        @pl.when(t < chunks)
        def _():
            wait_recv(fwd_recv(t))
            multiply(t, 0)

        @pl.when(jnp.logical_and(t >= 1, t - 1 < chunks))
        def _():
            c = t - 1
            core_copy(c).wait_recv()
            for a in range(XL):
                prod[c, a, z2, k] = prod[c, a, z2, k] + cr[c, a, z2]
            start(z1_copy(c))

        @pl.when(t < chunks)
        def _():
            multiply(t, 1)
            core_copy(t).start()

        @pl.when(jnp.logical_and(t >= LAG_Z2, t - LAG_Z2 < chunks))
        def _():
            c = t - LAG_Z2
            wait_recv(z1_copy(c))
            for a in range(XL):
                prod[c, a, zp, k, :, 0:half] = (
                    prod[c, a, zp, k, :, 0:half] + cr[c, a, zp, :, 0:half] + z1p[c, a])
                prod[c, a, zp, k, :, half:] = prod[c, a, zp, k, :, half:] + cr[c, a, zp, :, half:]
                prod[c, a, zm, k, :, 0:half] = prod[c, a, zm, k, :, 0:half] + cr[c, a, zm, :, 0:half]
                prod[c, a, zm, k, :, half:] = (
                    prod[c, a, zm, k, :, half:] + cr[c, a, zm, :, half:] + z1m[c, a])
            start(z2_copy(c))

        @pl.when(t == chunks + LAG_Z2 - 1)
        def _():
            find_columns()

        @pl.when(jnp.logical_and(t >= LAG_FIN, t - LAG_FIN < chunks))
        def _():
            c = t - LAG_FIN
            wait_recv(z2_copy(c))
            for a in range(XL):
                prod[c, a, z, k] = prod[c, a, z, k] + cr[c, a, z] + z2p[c, a] + z2m[c, a]
            xl_copy(c).start()

        @pl.when(t >= LAG_OUT)
        def _():
            c = t - LAG_OUT
            xl_copy(c).wait_recv()
            v = prod[c, xl, z, k] + xb[c]
            out[pl.ds(pl.multiple_of(c * 8, 8), 8), :] = v
            out_copy(c).start()
            total = jnp.sum(fold_lanes(v * in_center - jnp.abs(v) * in_radius), axis=1, keepdims=True)
            tb[...] += jnp.where(lane8 == row8 + c * 8, jnp.broadcast_to(total, (8, LANES)), 0.0)

        @pl.when(t == LAG_OUT + 1)
        def _():
            for h in range(2):
                @pl.when(n != 2 * s + h)
                def _(h=h):
                    shs_copy(h).start()

                @pl.when(n == 2 * s + h)
                def _(h=h):
                    sb[n] = shs[h]

        @pl.when(jnp.logical_and(t == LAG_OUT + 4, n // 2 == s))
        def _():
            shift_recv()
            total = sb[0]
            for j in range(1, NNEUR):
                total = total + sb[j]
            tb[...] += jnp.where(row8 == 0, total + bias16[pl.ds(n, 1), :], 0.0)

        return carry

    lax.fori_loop(0, chunks + LAG_OUT, iteration, 0)

    pb[s] = tb[...]

    def spec_at(dx, dy):
        return (xh + dx) % XH * Y + (y + dy) % Y

    def pb_copy(dx, dy, src):
        return pltpu.make_async_remote_copy(
            src_ref=pb.at[src], dst_ref=pb.at[src], send_sem=pb_s.at[dx * Y + dy],
            recv_sem=pb_r.at[dx * Y + dy], device_id=(spec_at(dx, dy), n), device_id_type=MESH)

    spec_steps = [(1, 2), (1, 1), (1, 3), (1, 0), (0, 2), (0, 1), (0, 3)]
    for dx, dy in spec_steps:
        pb_copy(dx, dy, s).start()
    for dx, dy in spec_steps:
        pb_copy(dx, dy, spec_at(-dx + XH, -dy + Y)).wait_recv()
    bound = pb[0]
    for j in range(1, NSPEC):
        bound = bound + pb[j]
    bound = jnp.broadcast_to(jnp.sum(bound, axis=0, keepdims=True), (8, LANES))
    bb[n] = bound
    lbound[...] = bound[0:1, 0:lbound.shape[1]]

    def neuron_at(dx, dz, dk):
        return (xl + dx) % XL * 2 * Z + (z + dz) % Z * 2 + (k + dk) % 2

    def bb_copy(dx, dz, dk, src):
        at = dx * 2 * Z + dz * 2 + dk
        return pltpu.make_async_remote_copy(
            src_ref=bb.at[src], dst_ref=bb.at[src], send_sem=bb_s.at[at], recv_sem=bb_r.at[at],
            device_id=(s, neuron_at(dx, dz, dk)), device_id_type=MESH)

    neuron_steps = [(dx, dz, dk) for dx, dz in ((1, 2), (1, 1), (1, 3), (0, 2), (1, 0), (0, 1), (0, 3), (0, 0))
                    for dk in (1, 0) if (dx, dz, dk) != (0, 0, 0)]
    for step in neuron_steps:
        bb_copy(*step, n).start()

    def sent(src, kind):
        pltpu.make_async_remote_copy(
            src_ref=src, dst_ref=src, send_sem=ssem.at[kind], recv_sem=rsem.at[0, kind],
            device_id=dev_core, device_id_type=MESH).wait_send()

    rest = pl.ds(LOOK_PAR, chunks - LOOK_PAR)
    sent(g.at[:, xh, y], S_XH)
    for kind in (S_OWN_P, S_OWN_M, S_PAR_P, S_PAR_M):
        sent(g.at[pl.ds(0, LOOK_PAR), xh, y], kind)
    for kind in (S_PAIR_P, S_PAIR_M):
        sent(g.at[rest, :, y], kind)
    for kind in (S_FWD_P, S_FWD_M):
        sent(g.at[:, :, y, 0], kind)
    sent(prod.at[:, :, :, 1 - k], S_CORE)
    for kind in (S_Z1_P, S_Z1_M):
        sent(prod.at[:, :, z2, k, :, pl.ds(0, half)], kind)
    for kind in (S_Z2_P, S_Z2_M):
        sent(prod.at[:, :, z, k], kind)
    sent(prod.at[:, 1 - xl, z, k], S_XL)
    pltpu.make_async_copy(out, coef, osem.at[0]).wait()
    for h in range(2):
        @pl.when(n != 2 * s + h)
        def _(h=h):
            shs_copy(h).wait_send()

    for dx, dz, dk in neuron_steps:
        bb_copy(dx, dz, dk, neuron_at(-dx + XL, -dz + Z, -dk + 2)).wait_recv()

    row = lax.broadcasted_iota(jnp.int32, (8, 4 * LANES), 0)

    def parts(first):
        v = jnp.concatenate([bb[first + i] for i in range(4)], axis=1)
        p1 = v.astype(BF16).astype(F32)
        p2 = (v - p1).astype(BF16).astype(F32)
        p3 = v - p1 - p2
        return jnp.where(row == 0, p1, jnp.where(row == 1, p2, jnp.where(row == 2, p3, 0.0)))

    for b in range(2):
        lhs = jnp.concatenate([parts(8 * b), parts(8 * b + 4)], axis=0).astype(BF16)
        picked = jnp.dot(lhs, onehot[b], preferred_element_type=F32)
        low_found = jnp.sum(picked[0:8], axis=0, keepdims=True)
        high_found = -jnp.sum(picked[8:16], axis=0, keepdims=True)
        hit = touched[b:b + 1, :] > 0.0
        low0, high0 = plow[b:b + 1, :], phigh[b:b + 1, :]
        new_low = jnp.where(hit, jnp.maximum(low0, low_found), low0)
        new_high = jnp.where(hit, jnp.minimum(high0, high_found), high0)
        rising, falling = jnp.maximum(new_high, 0.0), jnp.maximum(-new_low, 0.0)
        unstable = jnp.logical_and(new_low < 0.0, new_high > 0.0)
        safe = jnp.where(unstable, rising + falling, 1.0)
        slope = jnp.where(new_low >= 0.0, 1.0, jnp.where(new_high <= 0.0, 0.0, rising / safe))
        nslope[b:b + 1, :] = slope
        nshift[b:b + 1, :] = slope * falling

    for dx, dy in spec_steps:
        pb_copy(dx, dy, s).wait_send()
    for step in neuron_steps:
        bb_copy(*step, n).wait_send()


def per_device(panel, weight, layer_bias, act_center, act_radius, alpha, in_center, in_radius,
               bias_in, spec_neuron, prior_lower, prior_upper):
    own_rows, kdim = panel.shape
    ndim = weight.shape[1]
    hrows = own_rows // 2
    chunks = hrows // 8
    spec_rows = bias_in.shape[0] // NNEUR
    vmem = pl.BlockSpec(memory_space=pltpu.VMEM)
    hbm = pl.BlockSpec(memory_space=pl.ANY)
    half = ndim // 2
    dma = pltpu.SemaphoreType.DMA
    small_in = (layer_bias.reshape(1, kdim), act_center, act_radius, alpha, in_center, in_radius,
                bias_in.reshape(-1, LANES), spec_neuron, prior_lower, prior_upper)
    results = pl.pallas_call(
        kernel,
        out_shape=(
            jax.ShapeDtypeStruct((hrows, ndim), F32),
            jax.ShapeDtypeStruct((1, spec_rows), F32),
            jax.ShapeDtypeStruct((2, kdim), F32),
            jax.ShapeDtypeStruct((2, kdim), F32),
        ),
        in_specs=[hbm] * 12,
        out_specs=(hbm, vmem, vmem, vmem),
        scratch_shapes=[pltpu.VMEM(a.shape, a.dtype) for a in small_in] + [
            pltpu.VMEM((2, hrows, kdim), F32),
            pltpu.VMEM((kdim // W_ROWS, W_ROWS, ndim), F32),
            pltpu.VMEM((kdim, ndim), BF16),
            pltpu.VMEM((kdim, ndim), BF16),
            pltpu.VMEM((chunks, XH, Y, 2, 8, kdim), F32),
            pltpu.VMEM((2 * 16 * NSPEC, kdim), BF16),
            pltpu.VMEM((chunks, XL, Z, 2, 8, ndim), F32),
            pltpu.VMEM((chunks, XL, Z, 8, ndim), F32),
            pltpu.VMEM((chunks, XL, 8, half), F32),
            pltpu.VMEM((chunks, XL, 8, half), F32),
            pltpu.VMEM((chunks, XL, 8, ndim), F32),
            pltpu.VMEM((chunks, XL, 8, ndim), F32),
            pltpu.VMEM((chunks, 8, ndim), F32),
            pltpu.VMEM((2, LANES, LANES), F32),
            pltpu.VMEM((8, LANES), F32),
            pltpu.VMEM((2, 8, LANES), F32),
            pltpu.VMEM((NNEUR, 8, LANES), F32),
            pltpu.VMEM((NSPEC, 8, LANES), F32),
            pltpu.VMEM((NNEUR, 8, LANES), F32),
            pltpu.VMEM((2, 4 * LANES, kdim), BF16),
            pltpu.VMEM((2, kdim), F32),
            pltpu.VMEM((NNEUR, LANES), F32),
            pltpu.VMEM((hrows, ndim), F32),
            dma((11 + kdim // W_ROWS,)), dma((1,)),
            dma((NCOPY,)), dma((chunks, NCOPY)),
            dma((2,)), dma((NNEUR,)),
            dma((NSPEC,)), dma((NSPEC,)),
            dma((NNEUR,)), dma((NNEUR,)),
        ],
        compiler_params=pltpu.CompilerParams(
            collective_id=0, has_side_effects=True, vmem_limit_bytes=60 * 1024 * 1024),
        cost_estimate=pl.CostEstimate(
            flops=6 * 8 * own_rows * kdim * ndim, bytes_accessed=4 * kdim * ndim, transcendentals=0),
    )(panel.reshape(2, hrows, kdim), weight, *small_in)
    coef, lbound, nslope, nshift = hand_on(results)
    return coef, lbound.reshape(spec_rows), nslope, nshift


def hand_on(arrays):
    count = len(arrays)
    parts = 6
    step = arrays[0].shape[0] // parts

    def copy_kernel(*refs):
        held = refs[2 * count:3 * count]
        sems_in, sems_out = refs[3 * count:]

        def moves(source, target, sems):
            pairs = [(source[0].at[pl.ds(i * step, step)], target[0].at[pl.ds(i * step, step)])
                     for i in range(parts)]
            pairs += [(source[i], target[i]) for i in range(1, count)]
            return [pltpu.make_async_copy(a, b, sems.at[i]) for i, (a, b) in enumerate(pairs)]

        into, outof = moves(refs[:count], held, sems_in), moves(held, refs[count:2 * count], sems_out)
        for copy in into:
            copy.start()
        for first, second in zip(into, outof):
            first.wait()
            second.start()
        for copy in outof:
            copy.wait()

    hbm = pl.BlockSpec(memory_space=pl.ANY)
    return pl.pallas_call(
        copy_kernel,
        out_shape=tuple(jax.ShapeDtypeStruct(a.shape, a.dtype) for a in arrays),
        in_specs=[hbm] * count,
        out_specs=(hbm,) * count,
        scratch_shapes=[pltpu.VMEM(a.shape, a.dtype) for a in arrays]
        + [pltpu.SemaphoreType.DMA((parts + count,))] * 2,
    )(*arrays)


def solution(mesh):
    in_specs = (
        P("spec", "neuron"),
        P("neuron", "spec"),
        P("neuron"),
        P(None, "neuron"),
        P(None, "neuron"),
        P(None, "neuron"),
        P(None, "spec"),
        P(None, "spec"),
        P(),
        P(),
        P(None, "neuron"),
        P(None, "neuron"),
    )
    out_specs = (P("neuron", "spec"), P("neuron"), P(None, "neuron"), P(None, "neuron"))
    return jax.shard_map(
        per_device, mesh=mesh, in_specs=in_specs, out_specs=out_specs, check_vma=False
    )
```
